256 devices in a mesh: sec: 4 (over y), tok: 16 (over x, z_hi, core), tp: 4 (over z_lo).
Axes of the slice: x: 4, y: 4, z: 8 (z_hi: 2, z_lo: 4; z = z_hi * 4 + z_lo), core: 2. Of those that a mesh axis runs over, the one named last changes fastest.
Arguments:
- roll_hidden: bfloat16 [32, 384, 8192], P('tok', None, 'tp')
- lengths: int32 [32], replicated, may hold values from 1 to 384, as said below
- norm_gain: float32 [4, 8192], P('sec'), may hold values from 0.1 to 1.9
- w_query: bfloat16 [4, 8192, 4096], P('sec', 'tok', 'tp')
- key_value_weight: bfloat16 [4, 8192, 2, 512], P('sec', 'tok', None, 'tp')
- score_head: float32 [4, 4096], P('sec', 'tp'), may hold values from -1.2 to 1.2
Outputs:
- joined: float32 [4, 6144], P(None, 'tok')
- advantage: float32 [6144], P('tok')
The draws below stay inside these ranges and needn't reach their ends.
Inputs may be any that keep to these rules, and one draw needn't show every extreme that they name: Rollouts 2 * j and 2 * j + 1 are the ones held by index j of tok. The lengths sum to 6144, and one rollout is exactly 384 long. The sum of the lengths of the rollouts held by indices below j differs from j * 384 by less than 192 for every j, and equals 575 for j = 1.
All inputs are finite; a program needn't handle non-finite values.
Results may differ from the reference program's by a relative error of at most 0.0035.
The reference program's roundings to bfloat16 on the way count: a program that leaves them out, or rounds other values in their place, can miss the bound.
Values may be sent and summed in bfloat16 or wider, within the bound.
A program may use at most 128 MiB of HBM per device.

```python
import math
import jax
import jax.numpy as jnp
from jax import lax

MODEL_WIDTH = 8192
QUERY_HEADS = 32
KEY_VALUE_HEADS = 4
HEAD_SIZE = 128
SECTION_COUNT = 4
ROLL_DEV = 2
LOCAL_TOKENS = 384
ROLLOUTS = 32
TOKENS = 6144
MAXLEN = 384


def shared_query_base(key):
    return jax.random.normal(jax.random.fold_in(key, 101), (SECTION_COUNT, MODEL_WIDTH, QUERY_HEADS * HEAD_SIZE), jnp.float32)


def draw_lengths(key, part):
    key = jax.random.fold_in(key, 11)
    key_drift, key_split = jax.random.split(key)
    devices_count = ROLLOUTS // ROLL_DEV
    half_rows = LOCAL_TOKENS // 2
    drift = jax.random.randint(key_drift, (devices_count + 1,), -(half_rows - 1), half_rows)
    marks = jnp.arange(devices_count + 1)
    drift = jnp.where((marks == 0) | (marks == devices_count), 0, drift)
    drift = jnp.where(marks == 1, half_rows - 1, drift)
    totals = LOCAL_TOKENS + drift[1:] - drift[:-1]
    lowest = jnp.maximum(1, totals - LOCAL_TOKENS)
    highest = jnp.minimum(LOCAL_TOKENS, totals - 1)
    first_len = jax.random.randint(key_split, (devices_count,), lowest, highest + 1)
    first_len = jnp.where(jnp.arange(devices_count) == 0, totals - LOCAL_TOKENS, first_len)
    second_len = totals - first_len
    return jnp.stack([first_len, second_len], axis=1).reshape(ROLLOUTS).astype(jnp.int32)


def draw_roll_hidden(key, part):
    key = jax.random.fold_in(key, 5)
    key_a = jax.random.fold_in(key, 0)
    value_rows = jax.random.normal(key_a, (ROLLOUTS, MAXLEN, MODEL_WIDTH), jnp.float32)
    return value_rows.astype(jnp.bfloat16)


def draw_w_query(key, part):
    start_offset = shared_query_base(key)
    return (start_offset * MODEL_WIDTH ** (-0.5)).astype(jnp.bfloat16)


def draw_key_value_weight(key, part):
    key = jax.random.fold_in(key, 9)
    padded_key_rows, padded_value_rows = jax.random.split(key)
    local_key_rows = jax.random.normal(padded_key_rows, (SECTION_COUNT, MODEL_WIDTH, KEY_VALUE_HEADS * HEAD_SIZE), jnp.float32)
    value_rows = jax.random.normal(padded_value_rows, (SECTION_COUNT, MODEL_WIDTH, KEY_VALUE_HEADS * HEAD_SIZE), jnp.float32)
    key_rows = local_key_rows
    return (jnp.stack([key_rows, value_rows], axis=2) * MODEL_WIDTH ** (-0.5)).astype(jnp.bfloat16)


def shard_levels(own_key, extent, pieces, low, top_value):
    loudness, own = 1.0, jax.random.fold_in(own_key, 6)
    for position, shards_of in pieces:
        heights = jnp.exp(jax.random.uniform(jax.random.fold_in(own, position), (shards_of,), jnp.float32, low / len(pieces), top_value / len(pieces)))
        loudness = loudness * jnp.repeat(heights, extent[position] // shards_of).reshape([-1 if axis == position else 1 for axis in range(len(extent))])
    return loudness


def centred(stream_key, shape, width, most, cuts=(), kind=jnp.bfloat16):
    loudness = shard_levels(stream_key, shape, cuts, -0.22, 0.18) if cuts else 1.0
    result = jax.random.normal(stream_key, shape, jnp.float32) * width * loudness
    return jnp.minimum(jnp.maximum(result, -most), most).astype(kind)


def setup_inputs(seed: int = 0) -> dict:
    key_list = jax.random.split(jax.random.key(seed), 7)
    return {
        "roll_hidden": draw_roll_hidden(jax.random.fold_in(key_list[6], 71), 0),
        "lengths": draw_lengths(jax.random.fold_in(key_list[6], 71), 0),
        "norm_gain": jnp.clip(1.0 + 0.18 * jax.random.normal(key_list[2], (SECTION_COUNT, MODEL_WIDTH), jnp.float32), 0.1, 1.9),
        "w_query": draw_w_query(jax.random.fold_in(key_list[6], 71), 0),
        "key_value_weight": draw_key_value_weight(jax.random.fold_in(key_list[6], 71), 0),
        "score_head": centred(key_list[5], (SECTION_COUNT, QUERY_HEADS * HEAD_SIZE), 0.2, 1.2, ((0, 4), (1, 4)), jnp.float32),
    }


EPSILON = 1e-05
KL_WEIGHT = 0.5

def pack_index(lengths):
    ends = jnp.cumsum(lengths).astype(jnp.int32)
    begins = (ends - lengths).astype(jnp.int32)
    packed_pos = jnp.arange(TOKENS, dtype=jnp.int32)
    owner = lax.optimization_barrier(jnp.sum((packed_pos[:, None] >= ends[None, :]).astype(jnp.int32), axis=1)).astype(jnp.int32)
    place = (packed_pos - begins[owner]).astype(jnp.int32)
    return (owner, place)

def attend(query_rows, key_rows, value_rows, q_owner, q_place, k_owner, k_place, head):
    query_count = query_rows.shape[0]
    key_count = key_rows.shape[0]
    query_group = QUERY_HEADS // KEY_VALUE_HEADS
    query_four_axes = query_rows.reshape(query_count, KEY_VALUE_HEADS, query_group, HEAD_SIZE).astype(jnp.float32)
    key_three_axes = key_rows.reshape(key_count, KEY_VALUE_HEADS, HEAD_SIZE).astype(jnp.float32)
    value_three_axes = value_rows.reshape(key_count, KEY_VALUE_HEADS, HEAD_SIZE).astype(jnp.float32)
    logits = jnp.einsum('qhgd,khd->hgqk', query_four_axes, key_three_axes) / math.sqrt(HEAD_SIZE)
    allowed = (q_owner[:, None] == k_owner[None, :]) & (k_place[None, :] <= q_place[:, None]) & (k_owner[None, :] >= 0)
    logits = jnp.where(allowed[None, None], logits, jnp.float32(-1e+30))
    peak = lax.optimization_barrier(jnp.max(logits, axis=-1, keepdims=True))
    expo = jnp.exp(logits - peak)
    probs = (expo / lax.optimization_barrier(jnp.sum(expo, axis=-1, keepdims=True))).astype(jnp.bfloat16)
    mixed = jnp.einsum('hgqk,khd->qhgd', probs.astype(jnp.float32), value_three_axes)
    return lax.optimization_barrier(jnp.sum(mixed.reshape(query_count, QUERY_HEADS * HEAD_SIZE) * head[None, :], axis=1))

def reference(roll_hidden, lengths, norm_gain, w_query, key_value_weight, score_head):
    owner, place = pack_index(lengths)
    packed = roll_hidden[owner, place]
    floats = packed.astype(jnp.float32)
    scale = lax.rsqrt(lax.optimization_barrier(jnp.mean(floats * floats, axis=1, keepdims=True)) + EPSILON)
    blocks = TOKENS // LOCAL_TOKENS
    pad_owner = jnp.concatenate([-jnp.ones((LOCAL_TOKENS,), jnp.int32), owner])
    pad_place = jnp.concatenate([jnp.zeros((LOCAL_TOKENS,), jnp.int32), place])
    scores = []
    for section_index in range(SECTION_COUNT):
        normalized_rows = (floats * scale * norm_gain[section_index][None, :]).astype(jnp.bfloat16)
        query = jnp.dot(normalized_rows, w_query[section_index], preferred_element_type=jnp.float32).astype(jnp.bfloat16)
        key_value_pair = jnp.dot(normalized_rows, key_value_weight[section_index].reshape(MODEL_WIDTH, 2 * KEY_VALUE_HEADS * HEAD_SIZE), preferred_element_type=jnp.float32).astype(jnp.bfloat16)
        key_rows = key_value_pair[:, :KEY_VALUE_HEADS * HEAD_SIZE]
        value_rows = key_value_pair[:, KEY_VALUE_HEADS * HEAD_SIZE:]
        key_padding = jnp.concatenate([jnp.zeros((LOCAL_TOKENS, KEY_VALUE_HEADS * HEAD_SIZE), jnp.bfloat16), key_rows])
        value_padding = jnp.concatenate([jnp.zeros((LOCAL_TOKENS, KEY_VALUE_HEADS * HEAD_SIZE), jnp.bfloat16), value_rows])
        head = score_head[section_index]

        def one_block(block_index):
            first_row = (block_index * LOCAL_TOKENS).astype(jnp.int32)
            q_block = lax.dynamic_slice_in_dim(query, first_row, LOCAL_TOKENS, 0)
            q_owner = lax.dynamic_slice_in_dim(owner, first_row, LOCAL_TOKENS, 0)
            q_place = lax.dynamic_slice_in_dim(place, first_row, LOCAL_TOKENS, 0)
            k_block = lax.dynamic_slice_in_dim(key_padding, first_row, 2 * LOCAL_TOKENS, 0)
            v_block = lax.dynamic_slice_in_dim(value_padding, first_row, 2 * LOCAL_TOKENS, 0)
            k_owner = lax.dynamic_slice_in_dim(pad_owner, first_row, 2 * LOCAL_TOKENS, 0)
            k_place = lax.dynamic_slice_in_dim(pad_place, first_row, 2 * LOCAL_TOKENS, 0)
            return attend(q_block, k_block, v_block, q_owner, q_place, k_owner, k_place, head)
        per_block = lax.map(one_block, jnp.arange(blocks, dtype=jnp.int32))
        scores.append(per_block.reshape(TOKENS))
    joined = jnp.stack(scores, axis=0)
    advantage = joined[1] - joined[2] - KL_WEIGHT * (joined[3] - joined[0])
    return (joined, advantage)
```

```python
import math

import jax
import jax.numpy as jnp
from jax import lax
from jax.experimental import pallas as pl
from jax.experimental.pallas import tpu as pltpu
from jax.sharding import PartitionSpec as P

HEAD_SIZE = 128
LOCAL_TOKENS = 384
HALF = LOCAL_TOKENS // 2
EPSILON = 1e-05
KL_WEIGHT = 0.5
MESH = pl.DeviceIdType.MESH

SEC = 4
TOK = 16
TP = 4
WIDTH = 8192
PIECE = 512
COLS = 256
CHUNKS = 5
BLOCK = 128
NEG = -1e30
SENDS = 15


def kernel(
    len_ref, x_ref, gain_ref, wq_ref, wkv_ref, head_ref,
    joined_ref, adv_ref,
    w, xs, ext, halo, a, an, ss, scale, bias, acc, qb, kv, oacc, parts,
    x_sem, w_sem, ws, wr, a_s, a_r, h_s, h_r, kv_s, kv_r, p_s, p_r,
):
    y = lax.axis_index("sec")
    tok = lax.axis_index("tok")
    k = lax.axis_index("tp")
    xx = tok // 4
    h = (tok // 2) % 2
    c = tok % 2
    d = 2 * c - 1
    group = y * 4 + k

    def tok_at(x_, h_, c_):
        return x_ * 4 + h_ * 2 + c_

    xd = (xx + d + 4) % 4
    xo = (xx - d + 4) % 4
    x2 = (xx + 2) % 4
    to_xd = (y, tok_at(xd, h, c), k)
    to_xo = (y, tok_at(xo, h, c), k)
    to_z = (y, tok_at(xx, 1 - h, c), k)
    to_sib = (y, tok_at(xx, h, 1 - c), k)
    to_next = (y, (tok + 1) % TOK, k)
    to_prev = (y, (tok + TOK - 1) % TOK, k)
    k1 = k + 1 - 2 * (k % 2)
    k2 = (k + 2) % 4
    k3 = 3 - k
    yd = (y + d + 4) % 4
    yo = (y - d + 4) % 4
    y2 = (y + 2) % 4
    to_yd = (yd, tok, k)
    to_yo = (yo, tok, k)

    xcopies = [
        pltpu.make_async_copy(
            x_ref.at[i, :, pl.ds(pl.multiple_of(y * PIECE, PIECE), PIECE)], xs.at[i], x_sem.at[i]
        )
        for i in range(2)
    ]
    wcopies = [pltpu.make_async_copy(wkv_ref, w.at[0, tok], w_sem.at[0])]
    for n in range(1, CHUNKS):
        wcopies.append(
            pltpu.make_async_copy(
                wq_ref.at[0, :, pl.ds((n - 1) * COLS, COLS)], w.at[n, tok], w_sem.at[n]
            )
        )
    for cp in wcopies[:1] + xcopies + wcopies[1:]:
        cp.start()

    barrier = pltpu.get_barrier_semaphore()
    for dev in (to_xd, to_xo, to_z, to_sib, to_next, to_prev):
        pl.semaphore_signal(barrier, inc=1, device_id=dev, device_id_type=MESH)

    def greet(i, carry):
        g = (group + i) % 16
        pl.semaphore_signal(barrier, inc=1, device_id=(g // 4, tok, g % 4), device_id_type=MESH)
        return carry

    lax.fori_loop(1, 16, greet, 0)
    pl.semaphore_wait(barrier, 21)

    def wcopy(n, s, slot, dev):
        return pltpu.make_async_remote_copy(
            src_ref=w.at[n, s], dst_ref=w.at[n, s], send_sem=ws.at[n, slot], recv_sem=wr.at[n, s],
            device_id=dev, device_id_type=MESH,
        )

    def wsend(n, s, slot, dev):
        wcopy(n, s, slot, dev).start()

    def wwait(n, s):
        wcopy(n, s, 0, to_sib).wait_recv()

    def own_x(n):
        wcopies[n].wait()
        wsend(n, tok, 0, to_xd)
        wsend(n, tok, 1, to_xo)

    def own_sib(n):
        wsend(n, tok, 2, to_sib)

    def own_z(n):
        wsend(n, tok, 3, to_z)

    def ring1(n, h_, base):
        s = tok_at(xd, h_, c)
        wwait(n, s)
        wsend(n, s, base, to_xo)
        wsend(n, s, base + 1, to_sib)
        s = tok_at(xo, h_, c)
        wwait(n, s)
        wsend(n, s, base + 2, to_sib)

    def ring2(n, h_, base):
        s = tok_at(x2, h_, c)
        wwait(n, s)
        wsend(n, s, base + 3, to_sib)

    def own1(n):
        ring1(n, h, 7)

    def own2(n):
        ring2(n, h, 7)

    def part0(n):
        s = tok_at(xx, 1 - h, c)
        wwait(n, s)
        wsend(n, s, 4, to_xd)
        wsend(n, s, 5, to_xo)
        wsend(n, s, 6, to_sib)

    def part1(n):
        ring1(n, 1 - h, 11)

    def part2(n):
        ring2(n, 1 - h, 11)

    def sib_wait(n):
        def step(i, carry):
            wwait(n, i * 2 + 1 - c)
            return carry

        lax.fori_loop(0, 8, step, 0)

    def acopy(q, slot, dev):
        return pltpu.make_async_remote_copy(
            src_ref=a.at[q], dst_ref=a.at[q], send_sem=a_s.at[slot], recv_sem=a_r.at[q],
            device_id=dev, device_id_type=MESH,
        )

    def square(q):
        f = a[q].astype(jnp.float32)
        f = f * f
        ss[...] += (f[:, :128] + f[:, 128:256]) + (f[:, 256:384] + f[:, 384:])

    def a_y(q, slot):
        acopy(q, slot, to_yd).start()
        acopy(q, slot + 1, to_yo).start()

    def a_z(kk, slot):
        q = kk * 4 + y
        acopy(q, 0, to_yd).wait_recv()
        a_y(q, slot)
        square(q)

    def a_fwd(kk, slot):
        q = kk * 4 + yd
        acopy(q, 0, to_yd).wait_recv()
        acopy(q, slot, to_yo).start()
        square(q)

    def a_last(kk, yy):
        q = kk * 4 + yy
        acopy(q, 0, to_yd).wait_recv()
        square(q)

    own_x(0)
    own_z(0)
    own_sib(0)
    own_x(1)

    begin0 = jnp.int32(0)
    for r in range(2 * TOK):
        begin0 = begin0 + jnp.where(r < 2 * tok, len_ref[r], 0)
    len0 = len_ref[2 * tok]
    len1 = len_ref[2 * tok + 1]
    off0 = begin0 - (tok * LOCAL_TOKENS - HALF)
    off1 = off0 + len0
    for cp in xcopies:
        cp.wait()
    for rb in range(4):
        rows = lax.broadcasted_iota(jnp.int32, (HALF, LOCAL_TOKENS), 0) + rb * HALF
        place = lax.broadcasted_iota(jnp.int32, (HALF, LOCAL_TOKENS), 1)
        diff = rows - place
        e0 = jnp.where((diff == off0) & (place < len0), 1.0, 0.0).astype(jnp.bfloat16)
        e1 = jnp.where((diff == off1) & (place < len1), 1.0, 0.0).astype(jnp.bfloat16)
        both = jnp.dot(e0, xs[0], preferred_element_type=jnp.float32)
        both = both + jnp.dot(e1, xs[1], preferred_element_type=jnp.float32)
        ext[rb] = both.astype(jnp.bfloat16)

    def hcopy(src, dst, dev):
        return pltpu.make_async_remote_copy(
            src_ref=ext.at[src], dst_ref=halo.at[dst], send_sem=h_s.at[dst], recv_sem=h_r.at[dst],
            device_id=dev, device_id_type=MESH,
        )

    to_right = hcopy(3, 0, to_next)
    to_left = hcopy(0, 1, to_prev)
    to_right.start()
    to_left.start()
    ss[...] = jnp.zeros_like(ss)
    oacc[...] = jnp.zeros_like(oacc)

    own1(0)
    own_x(2)
    own_sib(1)

    to_right.wait_recv()
    to_left.wait_recv()
    mine = k * 4 + y
    a[mine, :HALF] = ext[1] + halo[0]
    a[mine, HALF:] = ext[2] + halo[1]
    acopy(mine, 0, (y, tok, k1)).start()
    acopy(mine, 1, (y, tok, k2)).start()
    acopy(mine, 2, (y, tok, k3)).start()
    a_y(mine, 3)
    own_z(1)
    square(mine)

    def bias_block(i, carry):
        t = tok * LOCAL_TOKENS + i * BLOCK + lax.broadcasted_iota(jnp.int32, (BLOCK, BLOCK), 0)
        start = jnp.zeros((BLOCK, BLOCK), jnp.int32)
        begin = jnp.int32(0)
        for r in range(2 * TOK):
            start = jnp.where(begin <= t, begin, start)
            begin = begin + len_ref[r]
        for j in range(4):
            u = (
                (tok - 1) * LOCAL_TOKENS + i * BLOCK + j * BLOCK
                + lax.broadcasted_iota(jnp.int32, (BLOCK, BLOCK), 1)
            )
            seen = (u <= t) & (u >= start)
            bias[i, :, j * BLOCK : (j + 1) * BLOCK] = jnp.where(seen, 0.0, NEG)
        return carry

    lax.fori_loop(0, 3, bias_block, 0)

    own2(0)
    own1(1)
    own_x(3)
    own_sib(2)
    a_z(k1, 5)
    own2(1)
    own1(2)
    own_x(4)
    part0(0)
    own_z(2)
    a_z(k2, 7)
    own_sib(3)
    own2(2)
    part1(0)
    own1(3)
    a_fwd(k, 11)
    a_z(k3, 9)
    own_z(3)
    own_sib(4)
    part2(0)
    own2(3)
    own1(4)
    part0(1)
    a_fwd(k1, 12)
    own_z(4)
    own2(4)
    part1(1)
    a_fwd(k2, 13)
    part2(1)
    a_last(k, yo)
    a_last(k, y2)
    a_fwd(k3, 14)
    part0(2)
    a_last(k1, yo)
    a_last(k1, y2)
    a_last(k2, yo)
    a_last(k2, y2)
    part1(2)
    a_last(k3, yo)
    a_last(k3, y2)

    total = jnp.sum(ss[...], axis=1, keepdims=True)
    scale[...] = jnp.broadcast_to(lax.rsqrt(total * (1.0 / WIDTH) + EPSILON), scale.shape)

    def norm(q, carry):
        g = gain_ref[:, pl.ds(pl.multiple_of(q * PIECE, PIECE), PIECE)]
        sc = scale[...]
        for j in range(4):
            cols = slice(j * 128, (j + 1) * 128)
            f = a[q, :, cols].astype(jnp.float32)
            an[q, :, cols] = (f * sc * g[:, cols]).astype(jnp.bfloat16)
        return carry

    lax.fori_loop(0, 16, norm, 0)

    def project(n):
        acc[...] = jnp.zeros_like(acc)

        def step(q, carry):
            acc[...] += jnp.dot(an[q], w[n, q], preferred_element_type=jnp.float32)
            return carry

        lax.fori_loop(0, 16, step, 0)

    def attend(n):
        qb[...] = acc[...].astype(jnp.bfloat16)
        for hh in range(2):
            weight = head_ref[:, (n - 1) * COLS + hh * HEAD_SIZE : (n - 1) * COLS + (hh + 1) * HEAD_SIZE]

            def block(i, carry):
                rows = pl.ds(pl.multiple_of(i * BLOCK, BLOCK), BLOCK)
                window = pl.ds(pl.multiple_of(i * BLOCK, BLOCK), 4 * BLOCK)
                s = lax.dot_general(
                    qb[rows, hh * HEAD_SIZE : (hh + 1) * HEAD_SIZE], kv[window, :HEAD_SIZE],
                    (((1,), (1,)), ((), ())), preferred_element_type=jnp.float32,
                )
                s = s * (1.0 / math.sqrt(HEAD_SIZE)) + bias[i]
                e = jnp.exp(s - jnp.max(s, axis=1, keepdims=True))
                p = (e * (1.0 / jnp.sum(e, axis=1, keepdims=True))).astype(jnp.bfloat16)
                o = jnp.dot(p, kv[window, HEAD_SIZE:], preferred_element_type=jnp.float32)
                oacc[rows] += o * weight
                return carry

            lax.fori_loop(0, 3, block, 0)

    sib_wait(0)
    project(0)
    kv[LOCAL_TOKENS:] = acc[...].astype(jnp.bfloat16)
    kv_copy = pltpu.make_async_remote_copy(
        src_ref=kv.at[pl.ds(LOCAL_TOKENS, LOCAL_TOKENS)], dst_ref=kv.at[pl.ds(0, LOCAL_TOKENS)],
        send_sem=kv_s.at[0], recv_sem=kv_r.at[0], device_id=to_next, device_id_type=MESH,
    )
    kv_copy.start()
    part2(2)
    part0(3)
    sib_wait(1)
    project(1)
    part1(3)
    kv_copy.wait_recv()
    attend(1)
    part2(3)
    part0(4)
    sib_wait(2)
    project(2)
    part1(4)
    attend(2)
    sib_wait(3)
    project(3)
    attend(3)
    part2(4)
    sib_wait(4)
    project(4)
    attend(4)

    parts[group] = jnp.sum(oacc[...].T, axis=0, keepdims=True)

    def pcopy(i, slot):
        g = (group + i) % 16
        return pltpu.make_async_remote_copy(
            src_ref=parts.at[group], dst_ref=parts.at[group], send_sem=p_s.at[i], recv_sem=p_r.at[slot],
            device_id=(g // 4, tok, g % 4), device_id_type=MESH,
        )

    def psend(i, carry):
        pcopy(i, group).start()
        return carry

    lax.fori_loop(1, 16, psend, 0)

    def pwait(i, carry):
        g = (group + i) % 16
        pltpu.make_async_remote_copy(
            src_ref=parts.at[g], dst_ref=parts.at[g], send_sem=p_s.at[i], recv_sem=p_r.at[g],
            device_id=(g // 4, tok, g % 4), device_id_type=MESH,
        ).wait_recv()
        return carry

    lax.fori_loop(1, 16, pwait, 0)
    score = [(parts[4 * s] + parts[4 * s + 1]) + (parts[4 * s + 2] + parts[4 * s + 3]) for s in range(SEC)]
    for s in range(SEC):
        joined_ref[s : s + 1] = score[s]
    adv_ref[...] = score[1] - score[2] - KL_WEIGHT * (score[3] - score[0])

    def drain(i, carry):
        wcopy(i // SENDS, tok, i % SENDS, to_sib).wait_send()
        return carry

    lax.fori_loop(0, CHUNKS * SENDS, drain, 0)

    def drain_a(i, carry):
        acopy(mine, i, to_yd).wait_send()
        return carry

    lax.fori_loop(0, 15, drain_a, 0)
    to_right.wait_send()
    to_left.wait_send()
    kv_copy.wait_send()

    def drain_p(i, carry):
        pcopy(i, group).wait_send()
        return carry

    lax.fori_loop(1, 16, drain_p, 0)


def local(roll_hidden, lengths, norm_gain, w_query, key_value_weight, score_head):
    vmem = pl.BlockSpec(memory_space=pltpu.VMEM)
    smem = pl.BlockSpec(memory_space=pltpu.SMEM)
    hbm = pl.BlockSpec(memory_space=pl.ANY)
    dma = pltpu.SemaphoreType.DMA
    bf16, f32 = jnp.bfloat16, jnp.float32
    joined, advantage = pl.pallas_call(
        kernel,
        out_shape=(
            jax.ShapeDtypeStruct((SEC, LOCAL_TOKENS), f32),
            jax.ShapeDtypeStruct((1, LOCAL_TOKENS), f32),
        ),
        in_specs=[smem, hbm, vmem, hbm, hbm, vmem],
        out_specs=(vmem, vmem),
        scratch_shapes=[
            pltpu.VMEM((CHUNKS, TOK, PIECE, COLS), bf16),
            pltpu.VMEM((2, LOCAL_TOKENS, PIECE), bf16),
            pltpu.VMEM((4, HALF, PIECE), bf16),
            pltpu.VMEM((2, HALF, PIECE), bf16),
            pltpu.VMEM((16, LOCAL_TOKENS, PIECE), bf16),
            pltpu.VMEM((16, LOCAL_TOKENS, PIECE), bf16),
            pltpu.VMEM((LOCAL_TOKENS, 128), f32),
            pltpu.VMEM((LOCAL_TOKENS, 128), f32),
            pltpu.VMEM((3, BLOCK, 4 * BLOCK), f32),
            pltpu.VMEM((LOCAL_TOKENS, COLS), f32),
            pltpu.VMEM((LOCAL_TOKENS, COLS), bf16),
            pltpu.VMEM((2 * LOCAL_TOKENS, COLS), bf16),
            pltpu.VMEM((LOCAL_TOKENS, HEAD_SIZE), f32),
            pltpu.VMEM((16, 1, LOCAL_TOKENS), f32),
            dma((2,)), dma((CHUNKS,)),
            dma((CHUNKS, SENDS)), dma((CHUNKS, TOK)),
            dma((15,)), dma((16,)),
            dma((2,)), dma((2,)),
            dma((1,)), dma((1,)),
            dma((16,)), dma((16,)),
        ],
        compiler_params=pltpu.CompilerParams(
            collective_id=0, has_side_effects=True, vmem_limit_bytes=56 * 1024 * 1024
        ),
        name="score_rollouts",
    )(
        lengths, roll_hidden, norm_gain, w_query,
        key_value_weight.reshape(PIECE, COLS), score_head,
    )
    return (joined, advantage.reshape(LOCAL_TOKENS))


def solution(mesh):
    in_specs = (
        P("tok", None, "tp"),
        P(),
        P("sec", None),
        P("sec", "tok", "tp"),
        P("sec", "tok", None, "tp"),
        P("sec", "tp"),
    )
    out_specs = (P(None, "tok"), P("tok"))
    return jax.shard_map(local, mesh=mesh, in_specs=in_specs, out_specs=out_specs, check_vma=False)
```

```python
import math

import jax
import jax.numpy as jnp
from jax import lax
from jax.experimental import pallas as pl
from jax.experimental.pallas import tpu as pltpu
from jax.sharding import PartitionSpec as P

HEAD_SIZE = 128
LOCAL_TOKENS = 384
HALF = LOCAL_TOKENS // 2
EPSILON = 1e-05
KL_WEIGHT = 0.5
MESH = pl.DeviceIdType.MESH

SEC = 4
TOK = 16
TP = 4
WIDTH = 8192
PIECE = 512
COLS = (256, 256, 256, 256, 128, 128)
CHUNKS = len(COLS)
BLOCK = 128
NEG = -1e30
SENDS = 15

ORDER = (
    ("halo",), ("oz", 0), ("ox", 1), ("ox", 0), ("hw",), ("o1", 1), ("ao", 2), ("ox", 3), ("ss",), ("ox", 2),
    ("ao", 1), ("o1", 3), ("os", 4), ("ay",), ("o1", 2), ("ao", 3), ("oz", 1), ("ox", 4), ("o2", 1), ("az", 2),
    ("o1", 4), ("o1b", 0), ("os", 2), ("ox", 5), ("p0", 0), ("sc",), ("o1b", 2), ("o1", 0), ("af", 2),
    ("az", 1), ("af", 1), ("nm", 0, "0"), ("o1b", 4), ("nm", 1, "o"), ("nm", 1, "d"), ("nm", 1, "0"), ("o1", 5),
    ("p1", 0), ("o2", 0), ("oz", 2), ("p0", 1), ("az", 3), ("os", 0), ("o1b", 1), ("nm", 1, "2"), ("p1b", 0),
    ("o1b", 3), ("p2", 0), ("af", 0), ("o2", 2), ("nm", 0, "o"), ("os", 3), ("oz", 3), ("nm", 2, "d"),
    ("p1", 1), ("af", 3), ("p0", 2), ("os", 1), ("nm", 2, "2"), ("nm", 3, "2"), ("nm", 3, "d"), ("p2", 1),
    ("oz", 4), ("o2", 3), ("nm", 3, "0"), ("nm", 0, "d"), ("nm", 2, "o"), ("nm", 2, "0"), ("nm", 3, "o"),
    ("nm", 0, "2"), ("p1", 2), ("pj", 0), ("kvs",), ("o2", 5), ("p0", 3), ("o2", 4), ("p1b", 2), ("os", 5),
    ("o1b", 5), ("p1b", 1), ("p0", 4), ("pj", 1), ("oz", 5), ("p1", 3), ("p2", 2), ("bias",), ("p1b", 3),
    ("p1", 4), ("at", 1), ("p2", 3), ("pj", 2), ("p1b", 4), ("p0", 5), ("p2", 4), ("at", 2), ("pj", 3),
    ("p1", 5), ("at", 3), ("pj", 4), ("p1b", 5), ("p2", 5), ("at", 4), ("z0",), ("pj", 5, 0, 0),
    ("pj", 5, 1, 0), ("pj", 5, 0, 1), ("pj", 5, 1, 1), ("at", 5),
)


def kernel(len_ref, x_ref, gain_ref, wq_ref, wkv_ref, head_ref, out_ref, *scratch):
    w = scratch[:CHUNKS]
    (
        kvw, xs, ext, halo, a, an, sq, scale, bias, acc, kv, oacc, parts,
        x_sem, w_sem, ws, wr, a_s, a_r, h_s, h_r, kv_s, kv_r, p_s, p_r, q_s, q_r,
    ) = scratch[CHUNKS:]
    y = lax.axis_index("sec")
    tok = lax.axis_index("tok")
    k = lax.axis_index("tp")
    xx = tok // 4
    h = (tok // 2) % 2
    c = tok % 2
    d = 2 * c - 1
    group = y * 4 + k

    def tok_at(x_, h_, c_):
        return x_ * 4 + h_ * 2 + c_

    xd = (xx + d + 4) % 4
    xo = (xx - d + 4) % 4
    x2 = (xx + 2) % 4
    to_xd = (y, tok_at(xd, h, c), k)
    to_xo = (y, tok_at(xo, h, c), k)
    to_z = (y, tok_at(xx, 1 - h, c), k)
    to_sib = (y, tok_at(xx, h, 1 - c), k)
    to_next = (y, (tok + 1) % TOK, k)
    to_prev = (y, (tok + TOK - 1) % TOK, k)
    k1 = k + 1 - 2 * (k % 2)
    k2 = (k + 2) % 4
    k3 = 3 - k
    yd = (y + d + 4) % 4
    yo = (y - d + 4) % 4
    y2 = (y + 2) % 4
    to_yd = (yd, tok, k)
    to_yo = (yo, tok, k)

    xcopies = [
        pltpu.make_async_copy(
            x_ref.at[i, :, pl.ds(pl.multiple_of(y * PIECE, PIECE), PIECE)], xs.at[i], x_sem.at[i]
        )
        for i in range(2)
    ]
    wcopies = [pltpu.make_async_copy(wkv_ref.at[0], kvw, w_sem.at[0])]
    for n in range(1, CHUNKS):
        wcopies.append(
            pltpu.make_async_copy(
                wq_ref.at[0, :, pl.ds(sum(COLS[1:n]), COLS[n])], w[n].at[tok], w_sem.at[n]
            )
        )
    for cp in xcopies + wcopies:
        cp.start()

    barrier = pltpu.get_barrier_semaphore()
    for dev in (to_xd, to_xo, to_z, to_sib, to_next, to_prev):
        pl.semaphore_signal(barrier, inc=1, device_id=dev, device_id_type=MESH)

    def greet(i, carry):
        g = (group + i) % 16
        pl.semaphore_signal(barrier, inc=1, device_id=(g // 4, tok, g % 4), device_id_type=MESH)
        return carry

    lax.fori_loop(1, 16, greet, 0)

    def wcopy(n, s, slot, dev):
        return pltpu.make_async_remote_copy(
            src_ref=w[n].at[s], dst_ref=w[n].at[s], send_sem=ws.at[n, slot], recv_sem=wr.at[n, s],
            device_id=dev, device_id_type=MESH,
        )

    def wsend(n, s, slot, dev):
        wcopy(n, s, slot, dev).start()

    def wwait(n, s):
        wcopy(n, s, 0, to_sib).wait_recv()

    def forward(n, h_, base):
        s = tok_at(xd, h_, c)
        wwait(n, s)
        wsend(n, s, base, to_xo)
        wsend(n, s, base + 1, to_sib)

    def near(n, h_, base):
        s = tok_at(xo, h_, c)
        wwait(n, s)
        wsend(n, s, base + 2, to_sib)

    def far(n, h_, base):
        s = tok_at(x2, h_, c)
        wwait(n, s)
        wsend(n, s, base + 3, to_sib)

    def acopy(q, slot, dev):
        return pltpu.make_async_remote_copy(
            src_ref=a.at[q], dst_ref=a.at[q], send_sem=a_s.at[slot], recv_sem=a_r.at[q],
            device_id=dev, device_id_type=MESH,
        )

    begin0 = jnp.int32(0)
    for r in range(2 * TOK):
        begin0 = begin0 + jnp.where(r < 2 * tok, len_ref[r], 0)
    len0 = len_ref[2 * tok]
    len1 = len_ref[2 * tok + 1]
    off0 = begin0 - (tok * LOCAL_TOKENS - HALF)
    off1 = off0 + len0
    for cp in xcopies:
        cp.wait()
    for rb in range(4):
        rows = lax.broadcasted_iota(jnp.int32, (HALF, LOCAL_TOKENS), 0) + rb * HALF
        place = lax.broadcasted_iota(jnp.int32, (HALF, LOCAL_TOKENS), 1)
        diff = rows - place
        e0 = jnp.where((diff == off0) & (place < len0), 1.0, 0.0).astype(jnp.bfloat16)
        e1 = jnp.where((diff == off1) & (place < len1), 1.0, 0.0).astype(jnp.bfloat16)
        both = jnp.dot(e0, xs[0], preferred_element_type=jnp.float32)
        both = both + jnp.dot(e1, xs[1], preferred_element_type=jnp.float32)
        ext[rb] = both.astype(jnp.bfloat16)

    for cp in wcopies:
        cp.wait()
    w[0][tok, :, :HEAD_SIZE] = kvw[:, 0]
    w[0][tok, :, HEAD_SIZE:] = kvw[:, 1]
    pl.semaphore_wait(barrier, 21)

    def hcopy(src, dst, dev):
        return pltpu.make_async_remote_copy(
            src_ref=ext.at[src], dst_ref=halo.at[dst], send_sem=h_s.at[dst], recv_sem=h_r.at[dst],
            device_id=dev, device_id_type=MESH,
        )

    to_right = hcopy(3, 0, to_next)
    to_left = hcopy(0, 1, to_prev)
    oacc[...] = jnp.zeros_like(oacc)
    mine = k * 4 + y

    def exchange(buf, send, recv):
        def copy(i, g, slot):
            to = (group + i) % 16
            return pltpu.make_async_remote_copy(
                src_ref=buf.at[g], dst_ref=buf.at[g], send_sem=send.at[i], recv_sem=recv.at[slot],
                device_id=(to // 4, tok, to % 4), device_id_type=MESH,
            )

        def start(i, carry):
            copy(i, group, group).start()
            return carry

        def wait(i, carry):
            g = (group + i) % 16
            copy(i, g, g).wait_recv()
            return carry

        def drain(i, carry):
            copy(i, group, group).wait_send()
            return carry

        return [lambda f=f: lax.fori_loop(1, 16, f, 0) for f in (start, wait, drain)]

    squares_start, squares_wait, squares_drain = exchange(sq, q_s, q_r)
    parts_start, parts_wait, parts_drain = exchange(parts, p_s, p_r)

    def norm(q):
        g = gain_ref[:, pl.ds(pl.multiple_of(q * PIECE, PIECE), PIECE)]

        def rows(i, carry):
            r = pl.ds(pl.multiple_of(i * 64, 64), 64)
            sc = scale[r]
            for j in range(4):
                cols = slice(j * 128, (j + 1) * 128)
                f = a[q, r, cols].astype(jnp.float32)
                an[q, r, cols] = (f * sc * g[:, cols]).astype(jnp.bfloat16)
            return carry

        lax.fori_loop(0, 6, rows, 0)

    def sib_wait(n):
        def step(i, carry):
            wwait(n, i * 2 + 1 - c)
            return carry

        lax.fori_loop(0, 8, step, 0)

    def shards(n, h_, c_):
        total = None
        for i in range(4):
            q = tok_at(i, h_, c_)
            part = jnp.dot(an[q], w[n][q], preferred_element_type=jnp.float32)
            total = part if total is None else total + part
        acc[:, : COLS[n]] += total

    def bias_block(i, carry):
        t = tok * LOCAL_TOKENS + i * BLOCK + lax.broadcasted_iota(jnp.int32, (BLOCK, BLOCK), 0)
        start = jnp.zeros((BLOCK, BLOCK), jnp.int32)
        begin = jnp.int32(0)
        for r in range(2 * TOK):
            start = jnp.where(begin <= t, begin, start)
            begin = begin + len_ref[r]
        for j in range(4):
            u = (
                (tok - 1) * LOCAL_TOKENS + i * BLOCK + j * BLOCK
                + lax.broadcasted_iota(jnp.int32, (BLOCK, BLOCK), 1)
            )
            seen = (u <= t) & (u >= start)
            bias[i, :, j * BLOCK : (j + 1) * BLOCK] = jnp.where(seen, 0.0, NEG)
        return carry


    def attend(n):
        lanes = [slice(j, j + HEAD_SIZE) for j in range(0, COLS[n], HEAD_SIZE)]
        base = sum(COLS[1:n])
        weights = [head_ref[:, base + j.start : base + j.stop] for j in lanes]
        for i in range(3):
            rows = slice(i * BLOCK, (i + 1) * BLOCK)
            window = slice(i * BLOCK, (i + 4) * BLOCK)
            q = jnp.concatenate([acc[rows, j] for j in lanes], axis=0)
            s = lax.dot_general(
                q.astype(jnp.bfloat16), kv[window, :HEAD_SIZE],
                (((1,), (1,)), ((), ())), preferred_element_type=jnp.float32,
            )
            s = s * (math.log2(math.e) / math.sqrt(HEAD_SIZE))
            seen = bias[i]
            s = jnp.concatenate([s[m * BLOCK : (m + 1) * BLOCK] + seen for m in range(len(lanes))], axis=0)
            e = jnp.exp2(s - jnp.max(s, axis=1, keepdims=True))
            p = (e * (1.0 / jnp.sum(e, axis=1, keepdims=True))).astype(jnp.bfloat16)
            o = jnp.dot(p, kv[window, HEAD_SIZE:], preferred_element_type=jnp.float32)
            oacc[rows] += sum(o[m * BLOCK : (m + 1) * BLOCK] * weights[m] for m in range(len(lanes)))

    pieces = (k, k1, k2, k3)
    kv_copy = pltpu.make_async_remote_copy(
        src_ref=kv.at[pl.ds(LOCAL_TOKENS, LOCAL_TOKENS)], dst_ref=kv.at[pl.ds(0, LOCAL_TOKENS)],
        send_sem=kv_s.at[0], recv_sem=kv_r.at[0], device_id=to_next, device_id_type=MESH,
    )

    class Steps:
        def ox(n):
            wsend(n, tok, 0, to_xd)
            wsend(n, tok, 1, to_xo)

        def oz(n):
            wsend(n, tok, 3, to_z)

        def os(n):
            wsend(n, tok, 2, to_sib)

        def o1(n):
            forward(n, h, 7)

        def o1b(n):
            near(n, h, 7)

        def o2(n):
            far(n, h, 7)

        def p0(n):
            s = tok_at(xx, 1 - h, c)
            wwait(n, s)
            wsend(n, s, 4, to_xd)
            wsend(n, s, 5, to_xo)
            wsend(n, s, 6, to_sib)

        def p1(n):
            forward(n, 1 - h, 11)

        def p1b(n):
            near(n, 1 - h, 11)

        def p2(n):
            far(n, 1 - h, 11)

        def halo():
            to_right.start()
            to_left.start()

        def hw():
            to_right.wait_recv()
            to_left.wait_recv()
            a[mine, :HALF] = ext[1] + halo[0]
            a[mine, HALF:] = ext[2] + halo[1]

        def ay():
            acopy(mine, 3, to_yd).start()
            acopy(mine, 4, to_yo).start()

        def ao(i):
            acopy(mine, i - 1, (y, tok, pieces[i])).start()

        def az(i):
            q = pieces[i] * 4 + y
            acopy(q, 0, to_yd).wait_recv()
            acopy(q, 3 + 2 * i, to_yd).start()
            acopy(q, 4 + 2 * i, to_yo).start()

        def af(i):
            q = pieces[i] * 4 + yd
            acopy(q, 0, to_yd).wait_recv()
            acopy(q, 11 + i, to_yo).start()

        def ss():
            total = jnp.zeros((LOCAL_TOKENS, 128), jnp.float32)
            for j in range(4):
                f = a[mine, :, j * 128 : (j + 1) * 128].astype(jnp.float32)
                total = total + f * f
            sq[group] = jnp.sum(total.T, axis=0, keepdims=True)
            squares_start()

        def sc():
            squares_wait()
            total = sq[0]
            for g in range(1, 16):
                total = total + sq[g]
            row = lax.rsqrt(total * (1.0 / WIDTH) + EPSILON)
            scale[...] = jnp.broadcast_to(row, (128, LOCAL_TOKENS)).T

        def nm(i, r):
            q = pieces[i] * 4 + {"0": y, "d": yd, "o": yo, "2": y2}[r]
            if r in "o2":
                acopy(q, 0, to_yd).wait_recv()
            norm(q)

        def bias():
            lax.fori_loop(0, 3, bias_block, 0)

        def pj(n, a_=None, b_=None):
            if a_ is None:
                acc[...] = jnp.zeros_like(acc)
                sib_wait(n)

                def step(i, carry):
                    shards(n, i // 2, i % 2)
                    return carry

                lax.fori_loop(0, 4, step, 0)
                return
            h_ = h + a_ - 2 * h * a_
            c_ = c + b_ - 2 * c * b_
            if b_ == 1:
                def wait(i, carry):
                    wwait(n, tok_at(i, h_, c_))
                    return carry

                lax.fori_loop(0, 4, wait, 0)
            shards(n, h_, c_)

        def z0():
            acc[...] = jnp.zeros_like(acc)

        def kvs():
            kv[LOCAL_TOKENS:] = acc[...].astype(jnp.bfloat16)
            kv_copy.start()

        def at(n):
            if n == 1:
                kv_copy.wait_recv()
            attend(n)

    for name, *args in ORDER:
        getattr(Steps, name)(*args)

    parts[group] = jnp.sum(oacc[...].T, axis=0, keepdims=True)
    parts_start()
    parts_wait()
    score = [(parts[4 * s] + parts[4 * s + 1]) + (parts[4 * s + 2] + parts[4 * s + 3]) for s in range(SEC)]
    for s in range(SEC):
        out_ref[s : s + 1] = score[s]
    out_ref[SEC : SEC + 1] = score[1] - score[2] - KL_WEIGHT * (score[3] - score[0])

    for n in range(CHUNKS):
        def drain(i, carry):
            wcopy(n, tok, i, to_sib).wait_send()
            return carry

        lax.fori_loop(0, SENDS, drain, 0)

    def drain_a(i, carry):
        acopy(mine, i, to_yd).wait_send()
        return carry

    lax.fori_loop(0, 15, drain_a, 0)
    to_right.wait_send()
    to_left.wait_send()
    kv_copy.wait_send()

    squares_drain()
    parts_drain()


def local(roll_hidden, lengths, norm_gain, w_query, key_value_weight, score_head):
    vmem = pl.BlockSpec(memory_space=pltpu.VMEM)
    smem = pl.BlockSpec(memory_space=pltpu.SMEM)
    hbm = pl.BlockSpec(memory_space=pl.ANY)
    dma = pltpu.SemaphoreType.DMA
    bf16, f32 = jnp.bfloat16, jnp.float32
    out = pl.pallas_call(
        kernel,
        out_shape=jax.ShapeDtypeStruct((SEC + 1, LOCAL_TOKENS), f32),
        in_specs=[smem, hbm, vmem, hbm, hbm, vmem],
        out_specs=vmem,
        scratch_shapes=[
            *(pltpu.VMEM((TOK, PIECE, cols), bf16) for cols in COLS),
            pltpu.VMEM((PIECE, 2, HEAD_SIZE), bf16),
            pltpu.VMEM((2, LOCAL_TOKENS, PIECE), bf16),
            pltpu.VMEM((4, HALF, PIECE), bf16),
            pltpu.VMEM((2, HALF, PIECE), bf16),
            pltpu.VMEM((16, LOCAL_TOKENS, PIECE), bf16),
            pltpu.VMEM((16, LOCAL_TOKENS, PIECE), bf16),
            pltpu.VMEM((16, 1, LOCAL_TOKENS), f32),
            pltpu.VMEM((LOCAL_TOKENS, 128), f32),
            pltpu.VMEM((3, BLOCK, 4 * BLOCK), f32),
            pltpu.VMEM((LOCAL_TOKENS, max(COLS)), f32),
            pltpu.VMEM((2 * LOCAL_TOKENS, 2 * HEAD_SIZE), bf16),
            pltpu.VMEM((LOCAL_TOKENS, HEAD_SIZE), f32),
            pltpu.VMEM((16, 1, LOCAL_TOKENS), f32),
            dma((2,)), dma((CHUNKS,)),
            dma((CHUNKS, SENDS)), dma((CHUNKS, TOK)),
            dma((15,)), dma((16,)),
            dma((2,)), dma((2,)),
            dma((1,)), dma((1,)),
            dma((16,)), dma((16,)),
            dma((16,)), dma((16,)),
        ],
        compiler_params=pltpu.CompilerParams(
            collective_id=0, has_side_effects=True, vmem_limit_bytes=56 * 1024 * 1024
        ),
        name="score_rollouts",
    )(
        lengths, roll_hidden, norm_gain, w_query,
        key_value_weight, score_head,
    )
    return (out[:SEC], out[SEC])


def solution(mesh):
    in_specs = (
        P("tok", None, "tp"),
        P(),
        P("sec", None),
        P("sec", "tok", "tp"),
        P("sec", "tok", None, "tp"),
        P("sec", "tp"),
    )
    out_specs = (P(None, "tok"), P("tok"))
    return jax.shard_map(local, mesh=mesh, in_specs=in_specs, out_specs=out_specs, check_vma=False)
```

```python
import math

import jax
import jax.numpy as jnp
from jax import lax
from jax.experimental import pallas as pl
from jax.experimental.pallas import tpu as pltpu
from jax.sharding import PartitionSpec as P

HEAD_SIZE = 128
LOCAL_TOKENS = 384
HALF = LOCAL_TOKENS // 2
EPSILON = 1e-05
KL_WEIGHT = 0.5
MESH = pl.DeviceIdType.MESH

SEC = 4
TOK = 16
TP = 4
WIDTH = 8192
PIECE = 512
COLS = (256, 256, 256, 256, 128, 128)
CHUNKS = len(COLS)
BLOCK = 128
NEG = -1e30
SENDS = 15

ORDER = (
    ("halo",), ("ox", 1), ("o1", 1), ("oz", 0), ("hw",), ("ox", 3), ("ao", 1), ("ao", 3), ("ox", 2), ("o1", 3),
    ("ay",), ("p0", 0), ("oz", 1), ("ao", 2), ("ox", 4), ("os", 4), ("ox", 5), ("o1", 4), ("o1", 2), ("o1b", 3),
    ("af", 0), ("az", 1), ("ss",), ("ox", 0), ("p0", 1), ("o1", 5), ("af", 1), ("az", 3), ("oz", 2), ("p1", 1),
    ("o2", 4), ("bias",), ("p1", 0), ("o1b", 0), ("sc",), ("az", 2), ("o1b", 5), ("o1", 0), ("o2", 5),
    ("nm", 0, "2"), ("oz", 3), ("os", 5), ("p0", 2), ("o2", 2), ("p1b", 1), ("p2", 0), ("af", 3),
    ("nm", 2, "0"), ("os", 3), ("p1b", 0), ("os", 2), ("nm", 0, "0"), ("o1b", 2), ("o2", 0), ("os", 1),
    ("o1b", 1), ("o1b", 4), ("af", 2), ("oz", 4), ("p1", 2), ("nm", 1, "0"), ("nm", 0, "o"), ("nm", 0, "d"),
    ("nm", 2, "o"), ("p1b", 2), ("o2", 1), ("os", 0), ("nm", 1, "2"), ("nm", 3, "o"), ("nm", 1, "o"), ("oz", 5),
    ("nm", 1, "d"), ("nm", 3, "d"), ("nm", 2, "d"), ("nm", 3, "2"), ("p0", 3), ("nm", 3, "0"), ("p2", 2),
    ("p2", 1), ("nm", 2, "2"), ("pj", 0), ("kvs",), ("p1", 3), ("p1b", 3), ("pj", 1), ("p0", 4), ("p0", 5),
    ("o2", 3), ("p2", 3), ("pj", 2), ("p1", 4), ("pj", 3), ("p1", 5), ("p1b", 4), ("kw",), ("at", 3),
    ("p1b", 5), ("p2", 4), ("at", 2), ("at", 1), ("p2", 5), ("pj", 4), ("z0",), ("at", 4), ("pj", 5, 1, 0),
    ("pj", 5, 0, 0), ("pj", 5, 1, 1), ("pj", 5, 0, 1), ("at", 5),
)


def kernel(len_ref, x_ref, gain_ref, wq_ref, wkv_ref, head_ref, out_ref, *scratch):
    w = scratch[:CHUNKS]
    (
        kvw, xs, ext, halo, a, an, sq, scale, bias, acc, qb, kv, oacc, parts,
        x_sem, w_sem, ws, wr, a_s, a_r, h_s, h_r, kv_s, kv_r, p_s, p_r, q_s, q_r,
    ) = scratch[CHUNKS:]
    y = lax.axis_index("sec")
    tok = lax.axis_index("tok")
    k = lax.axis_index("tp")
    xx = tok // 4
    h = (tok // 2) % 2
    c = tok % 2
    d = 2 * c - 1
    group = y * 4 + k

    def tok_at(x_, h_, c_):
        return x_ * 4 + h_ * 2 + c_

    xd = (xx + d + 4) % 4
    xo = (xx - d + 4) % 4
    x2 = (xx + 2) % 4
    to_xd = (y, tok_at(xd, h, c), k)
    to_xo = (y, tok_at(xo, h, c), k)
    to_z = (y, tok_at(xx, 1 - h, c), k)
    to_sib = (y, tok_at(xx, h, 1 - c), k)
    to_next = (y, (tok + 1) % TOK, k)
    to_prev = (y, (tok + TOK - 1) % TOK, k)
    k1 = k + 1 - 2 * (k % 2)
    k2 = (k + 2) % 4
    k3 = 3 - k
    yd = (y + d + 4) % 4
    yo = (y - d + 4) % 4
    y2 = (y + 2) % 4
    to_yd = (yd, tok, k)
    to_yo = (yo, tok, k)

    xcopies = [
        pltpu.make_async_copy(
            x_ref.at[i, :, pl.ds(pl.multiple_of(y * PIECE, PIECE), PIECE)], xs.at[i], x_sem.at[i]
        )
        for i in range(2)
    ]
    wcopies = [pltpu.make_async_copy(wkv_ref.at[0], kvw, w_sem.at[0])]
    for n in range(1, CHUNKS):
        wcopies.append(
            pltpu.make_async_copy(
                wq_ref.at[0, :, pl.ds(sum(COLS[1:n]), COLS[n])], w[n].at[tok], w_sem.at[n]
            )
        )
    for cp in xcopies + wcopies:
        cp.start()

    barrier = pltpu.get_barrier_semaphore()
    for dev in (to_xd, to_xo, to_z, to_sib, to_next, to_prev):
        pl.semaphore_signal(barrier, inc=1, device_id=dev, device_id_type=MESH)

    def greet(i, carry):
        g = (group + i) % 16
        pl.semaphore_signal(barrier, inc=1, device_id=(g // 4, tok, g % 4), device_id_type=MESH)
        return carry

    lax.fori_loop(1, 16, greet, 0)

    def wcopy(n, s, slot, dev):
        return pltpu.make_async_remote_copy(
            src_ref=w[n].at[s], dst_ref=w[n].at[s], send_sem=ws.at[n, slot], recv_sem=wr.at[n, s],
            device_id=dev, device_id_type=MESH,
        )

    def wsend(n, s, slot, dev):
        wcopy(n, s, slot, dev).start()

    def wwait(n, s):
        wcopy(n, s, 0, to_sib).wait_recv()

    def forward(n, h_, base):
        s = tok_at(xd, h_, c)
        wwait(n, s)
        wsend(n, s, base, to_xo)
        wsend(n, s, base + 1, to_sib)

    def near(n, h_, base):
        s = tok_at(xo, h_, c)
        wwait(n, s)
        wsend(n, s, base + 2, to_sib)

    def far(n, h_, base):
        s = tok_at(x2, h_, c)
        wwait(n, s)
        wsend(n, s, base + 3, to_sib)

    def acopy(q, slot, dev):
        return pltpu.make_async_remote_copy(
            src_ref=a.at[q], dst_ref=a.at[q], send_sem=a_s.at[slot], recv_sem=a_r.at[q],
            device_id=dev, device_id_type=MESH,
        )

    begin0 = jnp.int32(0)
    for r in range(2 * TOK):
        begin0 = begin0 + jnp.where(r < 2 * tok, len_ref[r], 0)
    len0 = len_ref[2 * tok]
    len1 = len_ref[2 * tok + 1]
    off0 = begin0 - (tok * LOCAL_TOKENS - HALF)
    off1 = off0 + len0
    for cp in xcopies:
        cp.wait()
    for rb in range(4):
        rows = lax.broadcasted_iota(jnp.int32, (HALF, LOCAL_TOKENS), 0) + rb * HALF
        place = lax.broadcasted_iota(jnp.int32, (HALF, LOCAL_TOKENS), 1)
        diff = rows - place
        e0 = jnp.where((diff == off0) & (place < len0), 1.0, 0.0).astype(jnp.bfloat16)
        e1 = jnp.where((diff == off1) & (place < len1), 1.0, 0.0).astype(jnp.bfloat16)
        both = jnp.dot(e0, xs[0], preferred_element_type=jnp.float32)
        both = both + jnp.dot(e1, xs[1], preferred_element_type=jnp.float32)
        ext[rb] = both.astype(jnp.bfloat16)

    for cp in wcopies:
        cp.wait()
    w[0][tok, :, :HEAD_SIZE] = kvw[:, 0]
    w[0][tok, :, HEAD_SIZE:] = kvw[:, 1]
    pl.semaphore_wait(barrier, 21)

    def hcopy(src, dst, dev):
        return pltpu.make_async_remote_copy(
            src_ref=ext.at[src], dst_ref=halo.at[dst], send_sem=h_s.at[dst], recv_sem=h_r.at[dst],
            device_id=dev, device_id_type=MESH,
        )

    to_right = hcopy(3, 0, to_next)
    to_left = hcopy(0, 1, to_prev)
    oacc[...] = jnp.zeros_like(oacc)
    mine = k * 4 + y

    def exchange(buf, send, recv):
        def copy(i, g, slot):
            to = (group + i) % 16
            return pltpu.make_async_remote_copy(
                src_ref=buf.at[g], dst_ref=buf.at[g], send_sem=send.at[i], recv_sem=recv.at[slot],
                device_id=(to // 4, tok, to % 4), device_id_type=MESH,
            )

        def start(i, carry):
            copy(i, group, group).start()
            return carry

        def wait(i, carry):
            g = (group + i) % 16
            copy(i, g, g).wait_recv()
            return carry

        def drain(i, carry):
            copy(i, group, group).wait_send()
            return carry

        return [lambda f=f: lax.fori_loop(1, 16, f, 0) for f in (start, wait, drain)]

    squares_start, squares_wait, squares_drain = exchange(sq, q_s, q_r)
    parts_start, parts_wait, parts_drain = exchange(parts, p_s, p_r)

    def norm(q):
        g = gain_ref[:, pl.ds(pl.multiple_of(q * PIECE, PIECE), PIECE)]

        def rows(i, carry):
            r = pl.ds(pl.multiple_of(i * 64, 64), 64)
            sc = scale[r]
            for j in range(4):
                cols = slice(j * 128, (j + 1) * 128)
                f = a[q, r, cols].astype(jnp.float32)
                an[q, r, cols] = (f * sc * g[:, cols]).astype(jnp.bfloat16)
            return carry

        lax.fori_loop(0, 6, rows, 0)

    def sib_wait(n):
        def step(i, carry):
            wwait(n, i * 2 + 1 - c)
            return carry

        lax.fori_loop(0, 8, step, 0)

    def shards(n, h_, c_):
        total = None
        for i in range(4):
            q = tok_at(i, h_, c_)
            part = jnp.dot(an[q], w[n][q], preferred_element_type=jnp.float32)
            total = part if total is None else total + part
        acc[:, : COLS[n]] += total

    def bias_block(i, carry):
        t = tok * LOCAL_TOKENS + i * BLOCK + lax.broadcasted_iota(jnp.int32, (BLOCK, BLOCK), 0)
        start = jnp.zeros((BLOCK, BLOCK), jnp.int32)
        begin = jnp.int32(0)
        for r in range(2 * TOK):
            start = jnp.where(begin <= t, begin, start)
            begin = begin + len_ref[r]
        for j in range(4):
            u = (
                (tok - 1) * LOCAL_TOKENS + i * BLOCK + j * BLOCK
                + lax.broadcasted_iota(jnp.int32, (BLOCK, BLOCK), 1)
            )
            seen = (u <= t) & (u >= start)
            bias[i, :, j * BLOCK : (j + 1) * BLOCK] = jnp.where(seen, 0.0, NEG)
        return carry


    def keep(n):
        base = sum(COLS[1:n])
        qb[:, base : base + COLS[n]] = acc[:, : COLS[n]].astype(jnp.bfloat16)

    def attend(n):
        lanes = [slice(j, j + HEAD_SIZE) for j in range(0, COLS[n], HEAD_SIZE)]
        base = sum(COLS[1:n])
        weights = [head_ref[:, base + j.start : base + j.stop] for j in lanes]
        for i in range(3):
            rows = slice(i * BLOCK, (i + 1) * BLOCK)
            window = slice(i * BLOCK, (i + 4) * BLOCK)
            q = jnp.concatenate([qb[rows, base + j.start : base + j.stop] for j in lanes], axis=0)
            s = lax.dot_general(
                q, kv[window, :HEAD_SIZE],
                (((1,), (1,)), ((), ())), preferred_element_type=jnp.float32,
            )
            s = s * (math.log2(math.e) / math.sqrt(HEAD_SIZE))
            seen = bias[i]
            s = jnp.concatenate([s[m * BLOCK : (m + 1) * BLOCK] + seen for m in range(len(lanes))], axis=0)
            e = jnp.exp2(s - jnp.max(s, axis=1, keepdims=True))
            p = (e * (1.0 / jnp.sum(e, axis=1, keepdims=True))).astype(jnp.bfloat16)
            o = jnp.dot(p, kv[window, HEAD_SIZE:], preferred_element_type=jnp.float32)
            oacc[rows] += sum(o[m * BLOCK : (m + 1) * BLOCK] * weights[m] for m in range(len(lanes)))

    pieces = (k, k1, k2, k3)
    kv_copy = pltpu.make_async_remote_copy(
        src_ref=kv.at[pl.ds(LOCAL_TOKENS, LOCAL_TOKENS)], dst_ref=kv.at[pl.ds(0, LOCAL_TOKENS)],
        send_sem=kv_s.at[0], recv_sem=kv_r.at[0], device_id=to_next, device_id_type=MESH,
    )

    class Steps:
        def ox(n):
            wsend(n, tok, 0, to_xd)
            wsend(n, tok, 1, to_xo)

        def oz(n):
            wsend(n, tok, 3, to_z)

        def os(n):
            wsend(n, tok, 2, to_sib)

        def o1(n):
            forward(n, h, 7)

        def o1b(n):
            near(n, h, 7)

        def o2(n):
            far(n, h, 7)

        def p0(n):
            s = tok_at(xx, 1 - h, c)
            wwait(n, s)
            wsend(n, s, 4, to_xd)
            wsend(n, s, 5, to_xo)
            wsend(n, s, 6, to_sib)

        def p1(n):
            forward(n, 1 - h, 11)

        def p1b(n):
            near(n, 1 - h, 11)

        def p2(n):
            far(n, 1 - h, 11)

        def halo():
            to_right.start()
            to_left.start()

        def hw():
            to_right.wait_recv()
            to_left.wait_recv()
            a[mine, :HALF] = ext[1] + halo[0]
            a[mine, HALF:] = ext[2] + halo[1]

        def ay():
            acopy(mine, 3, to_yd).start()
            acopy(mine, 4, to_yo).start()

        def ao(i):
            acopy(mine, i - 1, (y, tok, pieces[i])).start()

        def az(i):
            q = pieces[i] * 4 + y
            acopy(q, 0, to_yd).wait_recv()
            acopy(q, 3 + 2 * i, to_yd).start()
            acopy(q, 4 + 2 * i, to_yo).start()

        def af(i):
            q = pieces[i] * 4 + yd
            acopy(q, 0, to_yd).wait_recv()
            acopy(q, 11 + i, to_yo).start()

        def ss():
            total = jnp.zeros((LOCAL_TOKENS, 128), jnp.float32)
            for j in range(4):
                f = a[mine, :, j * 128 : (j + 1) * 128].astype(jnp.float32)
                total = total + f * f
            sq[group] = jnp.sum(total.T, axis=0, keepdims=True)
            squares_start()

        def sc():
            squares_wait()
            total = sq[0]
            for g in range(1, 16):
                total = total + sq[g]
            row = lax.rsqrt(total * (1.0 / WIDTH) + EPSILON)
            scale[...] = jnp.broadcast_to(row, (128, LOCAL_TOKENS)).T

        def nm(i, r):
            q = pieces[i] * 4 + {"0": y, "d": yd, "o": yo, "2": y2}[r]
            if r in "o2":
                acopy(q, 0, to_yd).wait_recv()
            norm(q)

        def bias():
            lax.fori_loop(0, 3, bias_block, 0)

        def pj(n, a_=None, b_=None):
            if a_ is None:
                acc[...] = jnp.zeros_like(acc)
                sib_wait(n)

                def step(i, carry):
                    shards(n, i // 2, i % 2)
                    return carry

                lax.fori_loop(0, 4, step, 0)
                if n > 0:
                    keep(n)
                return
            h_ = h + a_ - 2 * h * a_
            c_ = c + b_ - 2 * c * b_
            if b_ == 1:
                def wait(i, carry):
                    wwait(n, tok_at(i, h_, c_))
                    return carry

                lax.fori_loop(0, 4, wait, 0)
            shards(n, h_, c_)

        def z0():
            acc[...] = jnp.zeros_like(acc)

        def kw():
            kv_copy.wait_recv()

        def kvs():
            kv[LOCAL_TOKENS:] = acc[...].astype(jnp.bfloat16)
            kv_copy.start()

        def at(n):
            if n == CHUNKS - 1:
                keep(n)
            attend(n)

    for name, *args in ORDER:
        getattr(Steps, name)(*args)

    parts[group] = jnp.sum(oacc[...].T, axis=0, keepdims=True)
    parts_start()
    parts_wait()
    score = [(parts[4 * s] + parts[4 * s + 1]) + (parts[4 * s + 2] + parts[4 * s + 3]) for s in range(SEC)]
    for s in range(SEC):
        out_ref[s : s + 1] = score[s]
    out_ref[SEC : SEC + 1] = score[1] - score[2] - KL_WEIGHT * (score[3] - score[0])

    for n in range(CHUNKS):
        def drain(i, carry):
            wcopy(n, tok, i, to_sib).wait_send()
            return carry

        lax.fori_loop(0, SENDS, drain, 0)

    def drain_a(i, carry):
        acopy(mine, i, to_yd).wait_send()
        return carry

    lax.fori_loop(0, 15, drain_a, 0)
    to_right.wait_send()
    to_left.wait_send()
    kv_copy.wait_send()

    squares_drain()
    parts_drain()


def local(roll_hidden, lengths, norm_gain, w_query, key_value_weight, score_head):
    vmem = pl.BlockSpec(memory_space=pltpu.VMEM)
    smem = pl.BlockSpec(memory_space=pltpu.SMEM)
    hbm = pl.BlockSpec(memory_space=pl.ANY)
    dma = pltpu.SemaphoreType.DMA
    bf16, f32 = jnp.bfloat16, jnp.float32
    out = pl.pallas_call(
        kernel,
        out_shape=jax.ShapeDtypeStruct((SEC + 1, LOCAL_TOKENS), f32),
        in_specs=[smem, hbm, vmem, hbm, hbm, vmem],
        out_specs=vmem,
        scratch_shapes=[
            *(pltpu.VMEM((TOK, PIECE, cols), bf16) for cols in COLS),
            pltpu.VMEM((PIECE, 2, HEAD_SIZE), bf16),
            pltpu.VMEM((2, LOCAL_TOKENS, PIECE), bf16),
            pltpu.VMEM((4, HALF, PIECE), bf16),
            pltpu.VMEM((2, HALF, PIECE), bf16),
            pltpu.VMEM((16, LOCAL_TOKENS, PIECE), bf16),
            pltpu.VMEM((16, LOCAL_TOKENS, PIECE), bf16),
            pltpu.VMEM((16, 1, LOCAL_TOKENS), f32),
            pltpu.VMEM((LOCAL_TOKENS, 128), f32),
            pltpu.VMEM((3, BLOCK, 4 * BLOCK), f32),
            pltpu.VMEM((LOCAL_TOKENS, max(COLS)), f32),
            pltpu.VMEM((LOCAL_TOKENS, sum(COLS[1:])), bf16),
            pltpu.VMEM((2 * LOCAL_TOKENS, 2 * HEAD_SIZE), bf16),
            pltpu.VMEM((LOCAL_TOKENS, HEAD_SIZE), f32),
            pltpu.VMEM((16, 1, LOCAL_TOKENS), f32),
            dma((2,)), dma((CHUNKS,)),
            dma((CHUNKS, SENDS)), dma((CHUNKS, TOK)),
            dma((15,)), dma((16,)),
            dma((2,)), dma((2,)),
            dma((1,)), dma((1,)),
            dma((16,)), dma((16,)),
            dma((16,)), dma((16,)),
        ],
        compiler_params=pltpu.CompilerParams(
            collective_id=0, has_side_effects=True, vmem_limit_bytes=56 * 1024 * 1024
        ),
        name="score_rollouts",
    )(
        lengths, roll_hidden, norm_gain, w_query,
        key_value_weight, score_head,
    )
    return (out[:SEC], out[SEC])


def solution(mesh):
    in_specs = (
        P("tok", None, "tp"),
        P(),
        P("sec", None),
        P("sec", "tok", "tp"),
        P("sec", "tok", None, "tp"),
        P("sec", "tp"),
    )
    out_specs = (P(None, "tok"), P("tok"))
    return jax.shard_map(local, mesh=mesh, in_specs=in_specs, out_specs=out_specs, check_vma=False)
```

```python
import math

import jax
import jax.numpy as jnp
from jax import lax
from jax.experimental import pallas as pl
from jax.experimental.pallas import tpu as pltpu
from jax.sharding import PartitionSpec as P

HEAD_SIZE = 128
LOCAL_TOKENS = 384
HALF = LOCAL_TOKENS // 2
EPSILON = 1e-05
KL_WEIGHT = 0.5
MESH = pl.DeviceIdType.MESH

SEC = 4
TOK = 16
TP = 4
WIDTH = 8192
PIECE = 512
COLS = (256, 256, 256, 256, 256)
CHUNKS = len(COLS)
BLOCK = 128
NEG = -1e30
SENDS = 15

ORDER = (
    ("halo",), ("os", 4), ("ox", 4), ("ox", 2), ("ox", 1), ("oz", 1), ("ox", 0), ("oz", 0), ("hw",), ("ay",),
    ("o1", 4), ("o1", 0), ("os", 0), ("ao", 3), ("ao", 1), ("af", 0), ("p0", 0), ("o1b", 2), ("ao", 2),
    ("o2", 4), ("o1b", 0), ("o1b", 1), ("o1", 1), ("o1", 2), ("p0", 1), ("az", 1), ("os", 1), ("bias",),
    ("p1b", 0), ("os", 3), ("ss",), ("az", 3), ("af", 1), ("ox", 3), ("os", 2), ("p1", 1), ("oz", 2), ("o2", 0),
    ("p1", 0), ("o1", 3), ("sc",), ("az", 2), ("oz", 3), ("o2", 2), ("o2", 1), ("p0", 2), ("af", 2),
    ("nm", 1, "2"), ("nm", 2, "0"), ("o1b", 4), ("nm", 0, "0"), ("af", 3), ("nm", 0, "o"), ("nm", 2, "o"),
    ("o2", 3), ("nm", 1, "d"), ("nm", 0, "d"), ("oz", 4), ("p1b", 1), ("p2", 0), ("nm", 1, "0"), ("p2", 1),
    ("p1", 2), ("nm", 3, "d"), ("nm", 3, "o"), ("nm", 3, "0"), ("p0", 3), ("nm", 0, "2"), ("nm", 2, "d"),
    ("nm", 2, "2"), ("o1b", 3), ("p2", 2), ("nm", 3, "2"), ("p1b", 2), ("nm", 1, "o"), ("pj", 0), ("p1", 3),
    ("kvs",), ("pj", 1), ("p0", 4), ("p1b", 3), ("p2", 3), ("pj", 2), ("p1", 4), ("pj", 3), ("z0",), ("kw",),
    ("pj", 4, 0, 0), ("at", 1), ("p1b", 4), ("p2", 4), ("pj", 4, 1, 0), ("at", 2), ("pj", 4, 0, 1), ("at", 3),
    ("pj", 4, 1, 1), ("at", 4),
)


def kernel(len_ref, x_ref, gain_ref, wq_ref, wkv_ref, head_ref, out_ref, *scratch):
    w = scratch[:CHUNKS]
    (
        kvw, xs, ext, halo, a, an, sq, scale, bias, acc, qb, kv, oacc, parts,
        x_sem, w_sem, ws, wr, a_s, a_r, h_s, h_r, kv_s, kv_r, p_s, p_r, q_s, q_r,
    ) = scratch[CHUNKS:]
    y = lax.axis_index("sec")
    tok = lax.axis_index("tok")
    k = lax.axis_index("tp")
    xx = tok // 4
    h = (tok // 2) % 2
    c = tok % 2
    d = 2 * c - 1
    group = y * 4 + k

    def tok_at(x_, h_, c_):
        return x_ * 4 + h_ * 2 + c_

    xd = (xx + d + 4) % 4
    xo = (xx - d + 4) % 4
    x2 = (xx + 2) % 4
    to_xd = (y, tok_at(xd, h, c), k)
    to_xo = (y, tok_at(xo, h, c), k)
    to_z = (y, tok_at(xx, 1 - h, c), k)
    to_sib = (y, tok_at(xx, h, 1 - c), k)
    to_next = (y, (tok + 1) % TOK, k)
    to_prev = (y, (tok + TOK - 1) % TOK, k)
    k1 = k + 1 - 2 * (k % 2)
    k2 = (k + 2) % 4
    k3 = 3 - k
    yd = (y + d + 4) % 4
    yo = (y - d + 4) % 4
    y2 = (y + 2) % 4
    to_yd = (yd, tok, k)
    to_yo = (yo, tok, k)

    xcopies = [
        pltpu.make_async_copy(
            x_ref.at[i, :, pl.ds(pl.multiple_of(y * PIECE, PIECE), PIECE)], xs.at[i], x_sem.at[i]
        )
        for i in range(2)
    ]
    wcopies = [pltpu.make_async_copy(wkv_ref.at[0], kvw, w_sem.at[0])]
    for n in range(1, CHUNKS):
        wcopies.append(
            pltpu.make_async_copy(
                wq_ref.at[0, :, pl.ds(sum(COLS[1:n]), COLS[n])], w[n].at[tok], w_sem.at[n]
            )
        )
    for cp in xcopies + wcopies:
        cp.start()

    barrier = pltpu.get_barrier_semaphore()
    for dev in (to_xd, to_xo, to_z, to_sib, to_next, to_prev):
        pl.semaphore_signal(barrier, inc=1, device_id=dev, device_id_type=MESH)

    def greet(i, carry):
        g = (group + i) % 16
        pl.semaphore_signal(barrier, inc=1, device_id=(g // 4, tok, g % 4), device_id_type=MESH)
        return carry

    lax.fori_loop(1, 16, greet, 0)

    def wcopy(n, s, slot, dev):
        return pltpu.make_async_remote_copy(
            src_ref=w[n].at[s], dst_ref=w[n].at[s], send_sem=ws.at[n, slot], recv_sem=wr.at[n, s],
            device_id=dev, device_id_type=MESH,
        )

    def wsend(n, s, slot, dev):
        wcopy(n, s, slot, dev).start()

    def wwait(n, s):
        wcopy(n, s, 0, to_sib).wait_recv()

    def forward(n, h_, base):
        s = tok_at(xd, h_, c)
        wwait(n, s)
        wsend(n, s, base, to_xo)
        wsend(n, s, base + 1, to_sib)

    def near(n, h_, base):
        s = tok_at(xo, h_, c)
        wwait(n, s)
        wsend(n, s, base + 2, to_sib)

    def far(n, h_, base):
        s = tok_at(x2, h_, c)
        wwait(n, s)
        wsend(n, s, base + 3, to_sib)

    def acopy(q, slot, dev):
        return pltpu.make_async_remote_copy(
            src_ref=a.at[q], dst_ref=a.at[q], send_sem=a_s.at[slot], recv_sem=a_r.at[q],
            device_id=dev, device_id_type=MESH,
        )

    begin0 = jnp.int32(0)
    for r in range(2 * TOK):
        begin0 = begin0 + jnp.where(r < 2 * tok, len_ref[r], 0)
    len0 = len_ref[2 * tok]
    len1 = len_ref[2 * tok + 1]
    off0 = begin0 - (tok * LOCAL_TOKENS - HALF)
    off1 = off0 + len0
    for cp in xcopies:
        cp.wait()
    for rb in range(4):
        rows = lax.broadcasted_iota(jnp.int32, (HALF, LOCAL_TOKENS), 0) + rb * HALF
        place = lax.broadcasted_iota(jnp.int32, (HALF, LOCAL_TOKENS), 1)
        diff = rows - place
        e0 = jnp.where((diff == off0) & (place < len0), 1.0, 0.0).astype(jnp.bfloat16)
        e1 = jnp.where((diff == off1) & (place < len1), 1.0, 0.0).astype(jnp.bfloat16)
        both = jnp.dot(e0, xs[0], preferred_element_type=jnp.float32)
        both = both + jnp.dot(e1, xs[1], preferred_element_type=jnp.float32)
        ext[rb] = both.astype(jnp.bfloat16)

    for cp in wcopies:
        cp.wait()
    w[0][tok, :, :HEAD_SIZE] = kvw[:, 0]
    w[0][tok, :, HEAD_SIZE:] = kvw[:, 1]
    pl.semaphore_wait(barrier, 21)

    def hcopy(src, dst, dev):
        return pltpu.make_async_remote_copy(
            src_ref=ext.at[src], dst_ref=halo.at[dst], send_sem=h_s.at[dst], recv_sem=h_r.at[dst],
            device_id=dev, device_id_type=MESH,
        )

    to_right = hcopy(3, 0, to_next)
    to_left = hcopy(0, 1, to_prev)
    oacc[...] = jnp.zeros_like(oacc)
    mine = k * 4 + y

    def exchange(buf, send, recv):
        def copy(i, g, slot):
            to = (group + i) % 16
            return pltpu.make_async_remote_copy(
                src_ref=buf.at[g], dst_ref=buf.at[g], send_sem=send.at[i], recv_sem=recv.at[slot],
                device_id=(to // 4, tok, to % 4), device_id_type=MESH,
            )

        def start(i, carry):
            copy(i, group, group).start()
            return carry

        def wait(i, carry):
            g = (group + i) % 16
            copy(i, g, g).wait_recv()
            return carry

        def drain(i, carry):
            copy(i, group, group).wait_send()
            return carry

        return [lambda f=f: lax.fori_loop(1, 16, f, 0) for f in (start, wait, drain)]

    squares_start, squares_wait, squares_drain = exchange(sq, q_s, q_r)
    parts_start, parts_wait, parts_drain = exchange(parts, p_s, p_r)

    def norm(q):
        g = gain_ref[:, pl.ds(pl.multiple_of(q * PIECE, PIECE), PIECE)]

        def rows(i, carry):
            r = pl.ds(pl.multiple_of(i * 64, 64), 64)
            sc = scale[r]
            for j in range(4):
                cols = slice(j * 128, (j + 1) * 128)
                f = a[q, r, cols].astype(jnp.float32)
                an[q, r, cols] = (f * sc * g[:, cols]).astype(jnp.bfloat16)
            return carry

        lax.fori_loop(0, 6, rows, 0)

    def sib_wait(n):
        def step(i, carry):
            wwait(n, i * 2 + 1 - c)
            return carry

        lax.fori_loop(0, 8, step, 0)

    def shards(n, h_, c_):
        total = None
        for i in range(4):
            q = tok_at(i, h_, c_)
            part = jnp.dot(an[q], w[n][q], preferred_element_type=jnp.float32)
            total = part if total is None else total + part
        acc[:, : COLS[n]] += total

    def bias_block(i, carry):
        t = tok * LOCAL_TOKENS + i * BLOCK + lax.broadcasted_iota(jnp.int32, (BLOCK, BLOCK), 0)
        start = jnp.zeros((BLOCK, BLOCK), jnp.int32)
        begin = jnp.int32(0)
        for r in range(2 * TOK):
            start = jnp.where(begin <= t, begin, start)
            begin = begin + len_ref[r]
        for j in range(4):
            u = (
                (tok - 1) * LOCAL_TOKENS + i * BLOCK + j * BLOCK
                + lax.broadcasted_iota(jnp.int32, (BLOCK, BLOCK), 1)
            )
            seen = (u <= t) & (u >= start)
            bias[i, :, j * BLOCK : (j + 1) * BLOCK] = jnp.where(seen, 0.0, NEG)
        return carry


    def keep(n):
        base = sum(COLS[1:n])
        qb[:, base : base + COLS[n]] = acc[:, : COLS[n]].astype(jnp.bfloat16)

    def attend(n):
        lanes = [slice(j, j + HEAD_SIZE) for j in range(0, COLS[n], HEAD_SIZE)]
        base = sum(COLS[1:n])
        weights = [head_ref[:, base + j.start : base + j.stop] for j in lanes]
        for i in range(3):
            rows = slice(i * BLOCK, (i + 1) * BLOCK)
            window = slice(i * BLOCK, (i + 4) * BLOCK)
            q = jnp.concatenate([qb[rows, base + j.start : base + j.stop] for j in lanes], axis=0)
            s = lax.dot_general(
                q, kv[window, :HEAD_SIZE],
                (((1,), (1,)), ((), ())), preferred_element_type=jnp.float32,
            )
            s = s * (math.log2(math.e) / math.sqrt(HEAD_SIZE))
            seen = bias[i]
            s = jnp.concatenate([s[m * BLOCK : (m + 1) * BLOCK] + seen for m in range(len(lanes))], axis=0)
            e = jnp.exp2(s - jnp.max(s, axis=1, keepdims=True))
            p = (e * (1.0 / jnp.sum(e, axis=1, keepdims=True))).astype(jnp.bfloat16)
            o = jnp.dot(p, kv[window, HEAD_SIZE:], preferred_element_type=jnp.float32)
            oacc[rows] += sum(o[m * BLOCK : (m + 1) * BLOCK] * weights[m] for m in range(len(lanes)))

    pieces = (k, k1, k2, k3)
    kv_copy = pltpu.make_async_remote_copy(
        src_ref=kv.at[pl.ds(LOCAL_TOKENS, LOCAL_TOKENS)], dst_ref=kv.at[pl.ds(0, LOCAL_TOKENS)],
        send_sem=kv_s.at[0], recv_sem=kv_r.at[0], device_id=to_next, device_id_type=MESH,
    )

    class Steps:
        def ox(n):
            wsend(n, tok, 0, to_xd)
            wsend(n, tok, 1, to_xo)

        def oz(n):
            wsend(n, tok, 3, to_z)

        def os(n):
            wsend(n, tok, 2, to_sib)

        def o1(n):
            forward(n, h, 7)

        def o1b(n):
            near(n, h, 7)

        def o2(n):
            far(n, h, 7)

        def p0(n):
            s = tok_at(xx, 1 - h, c)
            wwait(n, s)
            wsend(n, s, 4, to_xd)
            wsend(n, s, 5, to_xo)
            wsend(n, s, 6, to_sib)

        def p1(n):
            forward(n, 1 - h, 11)

        def p1b(n):
            near(n, 1 - h, 11)

        def p2(n):
            far(n, 1 - h, 11)

        def halo():
            to_right.start()
            to_left.start()

        def hw():
            to_right.wait_recv()
            to_left.wait_recv()
            a[mine, :HALF] = ext[1] + halo[0]
            a[mine, HALF:] = ext[2] + halo[1]

        def ay():
            acopy(mine, 3, to_yd).start()
            acopy(mine, 4, to_yo).start()

        def ao(i):
            acopy(mine, i - 1, (y, tok, pieces[i])).start()

        def az(i):
            q = pieces[i] * 4 + y
            acopy(q, 0, to_yd).wait_recv()
            acopy(q, 3 + 2 * i, to_yd).start()
            acopy(q, 4 + 2 * i, to_yo).start()

        def af(i):
            q = pieces[i] * 4 + yd
            acopy(q, 0, to_yd).wait_recv()
            acopy(q, 11 + i, to_yo).start()

        def ss():
            total = jnp.zeros((LOCAL_TOKENS, 128), jnp.float32)
            for j in range(4):
                f = a[mine, :, j * 128 : (j + 1) * 128].astype(jnp.float32)
                total = total + f * f
            sq[group] = jnp.sum(total.T, axis=0, keepdims=True)
            squares_start()

        def sc():
            squares_wait()
            total = sq[0]
            for g in range(1, 16):
                total = total + sq[g]
            row = lax.rsqrt(total * (1.0 / WIDTH) + EPSILON)
            scale[...] = jnp.broadcast_to(row, (128, LOCAL_TOKENS)).T

        def nm(i, r):
            q = pieces[i] * 4 + {"0": y, "d": yd, "o": yo, "2": y2}[r]
            if r in "o2":
                acopy(q, 0, to_yd).wait_recv()
            norm(q)

        def bias():
            lax.fori_loop(0, 3, bias_block, 0)

        def pj(n, a_=None, b_=None):
            if a_ is None:
                acc[...] = jnp.zeros_like(acc)
                sib_wait(n)

                def step(i, carry):
                    shards(n, i // 2, i % 2)
                    return carry

                lax.fori_loop(0, 4, step, 0)
                if n > 0:
                    keep(n)
                return
            h_ = h + a_ - 2 * h * a_
            c_ = c + b_ - 2 * c * b_
            if b_ == 1:
                def wait(i, carry):
                    wwait(n, tok_at(i, h_, c_))
                    return carry

                lax.fori_loop(0, 4, wait, 0)
            shards(n, h_, c_)

        def z0():
            acc[...] = jnp.zeros_like(acc)

        def kw():
            kv_copy.wait_recv()

        def kvs():
            kv[LOCAL_TOKENS:] = acc[...].astype(jnp.bfloat16)
            kv_copy.start()

        def at(n):
            if n == CHUNKS - 1:
                keep(n)
            attend(n)

    for name, *args in ORDER:
        getattr(Steps, name)(*args)

    parts[group] = jnp.sum(oacc[...].T, axis=0, keepdims=True)
    parts_start()
    parts_wait()
    score = [(parts[4 * s] + parts[4 * s + 1]) + (parts[4 * s + 2] + parts[4 * s + 3]) for s in range(SEC)]
    for s in range(SEC):
        out_ref[s : s + 1] = score[s]
    out_ref[SEC : SEC + 1] = score[1] - score[2] - KL_WEIGHT * (score[3] - score[0])

    for n in range(CHUNKS):
        def drain(i, carry):
            wcopy(n, tok, i, to_sib).wait_send()
            return carry

        lax.fori_loop(0, SENDS, drain, 0)

    def drain_a(i, carry):
        acopy(mine, i, to_yd).wait_send()
        return carry

    lax.fori_loop(0, 15, drain_a, 0)
    to_right.wait_send()
    to_left.wait_send()
    kv_copy.wait_send()

    squares_drain()
    parts_drain()


def local(roll_hidden, lengths, norm_gain, w_query, key_value_weight, score_head):
    vmem = pl.BlockSpec(memory_space=pltpu.VMEM)
    smem = pl.BlockSpec(memory_space=pltpu.SMEM)
    hbm = pl.BlockSpec(memory_space=pl.ANY)
    dma = pltpu.SemaphoreType.DMA
    bf16, f32 = jnp.bfloat16, jnp.float32
    out = pl.pallas_call(
        kernel,
        out_shape=jax.ShapeDtypeStruct((SEC + 1, LOCAL_TOKENS), f32),
        in_specs=[smem, hbm, vmem, hbm, hbm, vmem],
        out_specs=vmem,
        scratch_shapes=[
            *(pltpu.VMEM((TOK, PIECE, cols), bf16) for cols in COLS),
            pltpu.VMEM((PIECE, 2, HEAD_SIZE), bf16),
            pltpu.VMEM((2, LOCAL_TOKENS, PIECE), bf16),
            pltpu.VMEM((4, HALF, PIECE), bf16),
            pltpu.VMEM((2, HALF, PIECE), bf16),
            pltpu.VMEM((16, LOCAL_TOKENS, PIECE), bf16),
            pltpu.VMEM((16, LOCAL_TOKENS, PIECE), bf16),
            pltpu.VMEM((16, 1, LOCAL_TOKENS), f32),
            pltpu.VMEM((LOCAL_TOKENS, 128), f32),
            pltpu.VMEM((3, BLOCK, 4 * BLOCK), f32),
            pltpu.VMEM((LOCAL_TOKENS, max(COLS)), f32),
            pltpu.VMEM((LOCAL_TOKENS, sum(COLS[1:])), bf16),
            pltpu.VMEM((2 * LOCAL_TOKENS, 2 * HEAD_SIZE), bf16),
            pltpu.VMEM((LOCAL_TOKENS, HEAD_SIZE), f32),
            pltpu.VMEM((16, 1, LOCAL_TOKENS), f32),
            dma((2,)), dma((CHUNKS,)),
            dma((CHUNKS, SENDS)), dma((CHUNKS, TOK)),
            dma((15,)), dma((16,)),
            dma((2,)), dma((2,)),
            dma((1,)), dma((1,)),
            dma((16,)), dma((16,)),
            dma((16,)), dma((16,)),
        ],
        compiler_params=pltpu.CompilerParams(
            collective_id=0, has_side_effects=True, vmem_limit_bytes=56 * 1024 * 1024
        ),
        name="score_rollouts",
    )(
        lengths, roll_hidden, norm_gain, w_query,
        key_value_weight, score_head,
    )
    return (out[:SEC], out[SEC])


def solution(mesh):
    in_specs = (
        P("tok", None, "tp"),
        P(),
        P("sec", None),
        P("sec", "tok", "tp"),
        P("sec", "tok", None, "tp"),
        P("sec", "tp"),
    )
    out_specs = (P(None, "tok"), P("tok"))
    return jax.shard_map(local, mesh=mesh, in_specs=in_specs, out_specs=out_specs, check_vma=False)
```

```python
import math

import jax
import jax.numpy as jnp
from jax import lax
from jax.experimental import pallas as pl
from jax.experimental.pallas import tpu as pltpu
from jax.sharding import PartitionSpec as P

HEAD_SIZE = 128
LOCAL_TOKENS = 384
HALF = LOCAL_TOKENS // 2
EPSILON = 1e-05
KL_WEIGHT = 0.5
MESH = pl.DeviceIdType.MESH

SEC = 4
TOK = 16
TP = 4
WIDTH = 8192
PIECE = 512
COLS = (256, 256, 256, 256, 256)
CHUNKS = len(COLS)
BLOCK = 128
NEG = -1e30
SENDS = 15

ORDER = (
    ("halo",), ("os", 4), ("ox", 4), ("ox", 2), ("ox", 1), ("oz", 1), ("ox", 0), ("oz", 0), ("hw",), ("ay",),
    ("o1", 4), ("o1", 0), ("os", 0), ("ao", 3), ("ao", 1), ("af", 0), ("p0", 0), ("o1b", 2), ("ao", 2),
    ("o2", 4), ("o1b", 0), ("o1b", 1), ("o1", 1), ("o1", 2), ("p0", 1), ("az", 1), ("os", 1), ("bias",),
    ("p1b", 0), ("os", 3), ("ss",), ("az", 3), ("af", 1), ("ox", 3), ("os", 2), ("p1", 1), ("oz", 2), ("o2", 0),
    ("p1", 0), ("o1", 3), ("sc",), ("az", 2), ("oz", 3), ("o2", 2), ("o2", 1), ("p0", 2), ("af", 2),
    ("nm", 1, "2"), ("nm", 2, "0"), ("o1b", 4), ("nm", 0, "0"), ("af", 3), ("nm", 0, "o"), ("nm", 2, "o"),
    ("o2", 3), ("nm", 1, "d"), ("nm", 0, "d"), ("oz", 4), ("p1b", 1), ("p2", 0), ("nm", 1, "0"), ("p2", 1),
    ("p1", 2), ("nm", 3, "d"), ("nm", 3, "o"), ("nm", 3, "0"), ("p0", 3), ("nm", 0, "2"), ("nm", 2, "d"),
    ("nm", 2, "2"), ("o1b", 3), ("p2", 2), ("nm", 3, "2"), ("p1b", 2), ("nm", 1, "o"), ("pj", 0), ("p1", 3),
    ("kvs",), ("pj", 1), ("p0", 4), ("p1b", 3), ("p2", 3), ("pj", 2), ("p1", 4), ("pj", 3), ("z0",), ("kw",),
    ("pj", 4, 0, 0), ("at", 1), ("p1b", 4), ("p2", 4), ("pj", 4, 1, 0), ("at", 2), ("pj", 4, 0, 1), ("at", 3),
    ("pj", 4, 1, 1), ("at", 4),
)


def kernel(len_ref, x_ref, gain_ref, wq_ref, wkv_ref, head_ref, out_ref, *scratch):
    w = scratch[:CHUNKS]
    (
        kvw, xs, ext, halo, a, an, sq, scale, bias, acc, qb, kv, oacc, parts,
        x_sem, w_sem, ws, wr, a_s, a_r, h_s, h_r, kv_s, kv_r, p_s, p_r, q_s, q_r,
    ) = scratch[CHUNKS:]
    y = lax.axis_index("sec")
    tok = lax.axis_index("tok")
    k = lax.axis_index("tp")
    xx = tok // 4
    h = (tok // 2) % 2
    c = tok % 2
    d = 2 * c - 1
    group = y * 4 + k

    def tok_at(x_, h_, c_):
        return x_ * 4 + h_ * 2 + c_

    xd = (xx + d + 4) % 4
    xo = (xx - d + 4) % 4
    x2 = (xx + 2) % 4
    to_xd = (y, tok_at(xd, h, c), k)
    to_xo = (y, tok_at(xo, h, c), k)
    to_z = (y, tok_at(xx, 1 - h, c), k)
    to_sib = (y, tok_at(xx, h, 1 - c), k)
    to_next = (y, (tok + 1) % TOK, k)
    to_prev = (y, (tok + TOK - 1) % TOK, k)
    k1 = k + 1 - 2 * (k % 2)
    k2 = (k + 2) % 4
    k3 = 3 - k
    yd = (y + d + 4) % 4
    yo = (y - d + 4) % 4
    y2 = (y + 2) % 4
    to_yd = (yd, tok, k)
    to_yo = (yo, tok, k)

    xcopies = [
        pltpu.make_async_copy(
            x_ref.at[i, :, pl.ds(pl.multiple_of(y * PIECE, PIECE), PIECE)], xs.at[i], x_sem.at[i]
        )
        for i in range(2)
    ]
    wcopies = [pltpu.make_async_copy(wkv_ref.at[0], kvw, w_sem.at[0])]
    for n in range(1, CHUNKS):
        wcopies.append(
            pltpu.make_async_copy(
                wq_ref.at[0, :, pl.ds(sum(COLS[1:n]), COLS[n])], w[n].at[tok], w_sem.at[n]
            )
        )
    for cp in xcopies + wcopies:
        cp.start()

    barrier = pltpu.get_barrier_semaphore()
    for dev in (to_xd, to_xo, to_z, to_sib, to_next, to_prev):
        pl.semaphore_signal(barrier, inc=1, device_id=dev, device_id_type=MESH)

    def greet(i, carry):
        g = (group + i) % 16
        pl.semaphore_signal(barrier, inc=1, device_id=(g // 4, tok, g % 4), device_id_type=MESH)
        return carry

    lax.fori_loop(1, 16, greet, 0)

    def wcopy(n, s, slot, dev):
        return pltpu.make_async_remote_copy(
            src_ref=w[n].at[s], dst_ref=w[n].at[s], send_sem=ws.at[n, slot], recv_sem=wr.at[n, s],
            device_id=dev, device_id_type=MESH,
        )

    def wsend(n, s, slot, dev):
        wcopy(n, s, slot, dev).start()

    def wwait(n, s):
        wcopy(n, s, 0, to_sib).wait_recv()

    def forward(n, h_, base):
        s = tok_at(xd, h_, c)
        wwait(n, s)
        wsend(n, s, base, to_xo)
        wsend(n, s, base + 1, to_sib)

    def near(n, h_, base):
        s = tok_at(xo, h_, c)
        wwait(n, s)
        wsend(n, s, base + 2, to_sib)

    def far(n, h_, base):
        s = tok_at(x2, h_, c)
        wwait(n, s)
        wsend(n, s, base + 3, to_sib)

    def acopy(q, slot, dev):
        return pltpu.make_async_remote_copy(
            src_ref=a.at[q], dst_ref=a.at[q], send_sem=a_s.at[slot], recv_sem=a_r.at[q],
            device_id=dev, device_id_type=MESH,
        )

    begin0 = jnp.int32(0)
    for r in range(2 * TOK):
        begin0 = begin0 + jnp.where(r < 2 * tok, len_ref[r], 0)
    len0 = len_ref[2 * tok]
    len1 = len_ref[2 * tok + 1]
    off0 = begin0 - (tok * LOCAL_TOKENS - HALF)
    off1 = off0 + len0
    for cp in xcopies:
        cp.wait()
    for rb in range(4):
        rows = lax.broadcasted_iota(jnp.int32, (HALF, LOCAL_TOKENS), 0) + rb * HALF
        place = lax.broadcasted_iota(jnp.int32, (HALF, LOCAL_TOKENS), 1)
        diff = rows - place
        e0 = jnp.where((diff == off0) & (place < len0), 1.0, 0.0).astype(jnp.bfloat16)
        e1 = jnp.where((diff == off1) & (place < len1), 1.0, 0.0).astype(jnp.bfloat16)
        both = jnp.dot(e0, xs[0], preferred_element_type=jnp.float32)
        both = both + jnp.dot(e1, xs[1], preferred_element_type=jnp.float32)
        ext[rb] = both.astype(jnp.bfloat16)

    for cp in wcopies:
        cp.wait()
    w[0][tok, :, :HEAD_SIZE] = kvw[:, 0]
    w[0][tok, :, HEAD_SIZE:] = kvw[:, 1]
    pl.semaphore_wait(barrier, 21)

    def hcopy(src, dst, dev):
        return pltpu.make_async_remote_copy(
            src_ref=ext.at[src], dst_ref=halo.at[dst], send_sem=h_s.at[dst], recv_sem=h_r.at[dst],
            device_id=dev, device_id_type=MESH,
        )

    to_right = hcopy(3, 0, to_next)
    to_left = hcopy(0, 1, to_prev)
    oacc[...] = jnp.zeros_like(oacc)
    mine = k * 4 + y

    def exchange(buf, send, recv):
        def copy(i, g, slot):
            to = (group + i) % 16
            return pltpu.make_async_remote_copy(
                src_ref=buf.at[g], dst_ref=buf.at[g], send_sem=send.at[i], recv_sem=recv.at[slot],
                device_id=(to // 4, tok, to % 4), device_id_type=MESH,
            )

        def start(i, carry):
            copy(i, group, group).start()
            return carry

        def wait(i, carry):
            g = (group + i) % 16
            copy(i, g, g).wait_recv()
            return carry

        def drain(i, carry):
            copy(i, group, group).wait_send()
            return carry

        return [lambda f=f: lax.fori_loop(1, 16, f, 0) for f in (start, wait, drain)]

    squares_start, squares_wait, squares_drain = exchange(sq, q_s, q_r)
    parts_start, parts_wait, parts_drain = exchange(parts, p_s, p_r)

    def norm(q):
        g = gain_ref[:, pl.ds(pl.multiple_of(q * PIECE, PIECE), PIECE)]

        def rows(i, carry):
            r = pl.ds(pl.multiple_of(i * 64, 64), 64)
            sc = scale[r]
            for j in range(4):
                cols = slice(j * 128, (j + 1) * 128)
                f = a[q, r, cols].astype(jnp.float32)
                an[q, r, cols] = (f * sc * g[:, cols]).astype(jnp.bfloat16)
            return carry

        lax.fori_loop(0, 6, rows, 0)

    def sib_wait(n):
        def step(i, carry):
            wwait(n, i * 2 + 1 - c)
            return carry

        lax.fori_loop(0, 8, step, 0)

    def shards(n, h_, c_):
        total = None
        for i in range(4):
            q = tok_at(i, h_, c_)
            part = jnp.dot(an[q], w[n][q], preferred_element_type=jnp.float32)
            total = part if total is None else total + part
        acc[:, : COLS[n]] += total

    def bias_block(i, carry):
        t = tok * LOCAL_TOKENS + i * BLOCK + lax.broadcasted_iota(jnp.int32, (BLOCK, BLOCK), 0)
        start = jnp.zeros((BLOCK, BLOCK), jnp.int32)
        begin = jnp.int32(0)
        for r in range(2 * TOK):
            start = jnp.where(begin <= t, begin, start)
            begin = begin + len_ref[r]
        for j in range(4):
            u = (
                (tok - 1) * LOCAL_TOKENS + i * BLOCK + j * BLOCK
                + lax.broadcasted_iota(jnp.int32, (BLOCK, BLOCK), 1)
            )
            seen = (u <= t) & (u >= start)
            bias[i, :, j * BLOCK : (j + 1) * BLOCK] = jnp.where(seen, 0.0, NEG)
        return carry


    def keep(n):
        base = sum(COLS[1:n])
        qb[:, base : base + COLS[n]] = acc[:, : COLS[n]].astype(jnp.bfloat16)

    def attend(n):
        lanes = [slice(j, j + HEAD_SIZE) for j in range(0, COLS[n], HEAD_SIZE)]
        base = sum(COLS[1:n])
        weights = [head_ref[:, base + j.start : base + j.stop] for j in lanes]
        for i in range(3):
            rows = slice(i * BLOCK, (i + 1) * BLOCK)
            window = slice(i * BLOCK, (i + 4) * BLOCK)
            q = jnp.concatenate([qb[rows, base + j.start : base + j.stop] for j in lanes], axis=0)
            s = lax.dot_general(
                q, kv[window, :HEAD_SIZE],
                (((1,), (1,)), ((), ())), preferred_element_type=jnp.float32,
            )
            s = s * (math.log2(math.e) / math.sqrt(HEAD_SIZE))
            seen = bias[i]
            s = jnp.concatenate([s[m * BLOCK : (m + 1) * BLOCK] + seen for m in range(len(lanes))], axis=0)
            e = jnp.exp2(s - jnp.max(s, axis=1, keepdims=True))
            p = (e * (1.0 / jnp.sum(e, axis=1, keepdims=True))).astype(jnp.bfloat16)
            o = jnp.dot(p, kv[window, HEAD_SIZE:], preferred_element_type=jnp.float32)
            oacc[rows] += sum(o[m * BLOCK : (m + 1) * BLOCK] * weights[m] for m in range(len(lanes)))

    pieces = (k, k1, k2, k3)
    kv_copy = pltpu.make_async_remote_copy(
        src_ref=kv.at[pl.ds(LOCAL_TOKENS, LOCAL_TOKENS)], dst_ref=kv.at[pl.ds(0, LOCAL_TOKENS)],
        send_sem=kv_s.at[0], recv_sem=kv_r.at[0], device_id=to_next, device_id_type=MESH,
    )

    class Steps:
        def ox(n):
            wsend(n, tok, 0, to_xd)
            wsend(n, tok, 1, to_xo)

        def oz(n):
            wsend(n, tok, 3, to_z)

        def os(n):
            wsend(n, tok, 2, to_sib)

        def o1(n):
            forward(n, h, 7)

        def o1b(n):
            near(n, h, 7)

        def o2(n):
            far(n, h, 7)

        def p0(n):
            s = tok_at(xx, 1 - h, c)
            wwait(n, s)
            wsend(n, s, 4, to_xd)
            wsend(n, s, 5, to_xo)
            wsend(n, s, 6, to_sib)

        def p1(n):
            forward(n, 1 - h, 11)

        def p1b(n):
            near(n, 1 - h, 11)

        def p2(n):
            far(n, 1 - h, 11)

        def halo():
            to_right.start()
            to_left.start()

        def hw():
            to_right.wait_recv()
            to_left.wait_recv()
            a[mine, :HALF] = ext[1] + halo[0]
            a[mine, HALF:] = ext[2] + halo[1]

        def ay():
            acopy(mine, 3, to_yd).start()
            acopy(mine, 4, to_yo).start()

        def ao(i):
            acopy(mine, i - 1, (y, tok, pieces[i])).start()

        def az(i):
            q = pieces[i] * 4 + y
            acopy(q, 0, to_yd).wait_recv()
            acopy(q, 3 + 2 * i, to_yd).start()
            acopy(q, 4 + 2 * i, to_yo).start()

        def af(i):
            q = pieces[i] * 4 + yd
            acopy(q, 0, to_yd).wait_recv()
            acopy(q, 11 + i, to_yo).start()

        def ss():
            total = jnp.zeros((LOCAL_TOKENS, 128), jnp.float32)
            for j in range(4):
                f = a[mine, :, j * 128 : (j + 1) * 128].astype(jnp.float32)
                total = total + f * f
            sq[group] = jnp.sum(total.T, axis=0, keepdims=True)
            squares_start()

        def sc():
            squares_wait()
            total = sq[0]
            for g in range(1, 16):
                total = total + sq[g]
            row = lax.rsqrt(total * (1.0 / WIDTH) + EPSILON)
            scale[...] = jnp.broadcast_to(row, (128, LOCAL_TOKENS)).T

        def nm(i, r):
            q = pieces[i] * 4 + {"0": y, "d": yd, "o": yo, "2": y2}[r]
            if r in "o2":
                acopy(q, 0, to_yd).wait_recv()
            norm(q)

        def bias():
            lax.fori_loop(0, 3, bias_block, 0)

        def pj(n, a_=None, b_=None):
            if a_ is None:
                acc[...] = jnp.zeros_like(acc)
                sib_wait(n)

                def step(i, carry):
                    shards(n, i // 2, i % 2)
                    return carry

                lax.fori_loop(0, 4, step, 0)
                if n > 0:
                    keep(n)
                return
            h_ = h + a_ - 2 * h * a_
            c_ = c + b_ - 2 * c * b_
            if b_ == 1:
                def wait(i, carry):
                    wwait(n, tok_at(i, h_, c_))
                    return carry

                lax.fori_loop(0, 4, wait, 0)
            shards(n, h_, c_)

        def z0():
            acc[...] = jnp.zeros_like(acc)

        def kw():
            kv_copy.wait_recv()

        def kvs():
            kv[LOCAL_TOKENS:] = acc[...].astype(jnp.bfloat16)
            kv_copy.start()

        def at(n):
            if n == CHUNKS - 1:
                keep(n)
            attend(n)

    for name, *args in ORDER:
        getattr(Steps, name)(*args)

    parts[group] = jnp.sum(oacc[...].T, axis=0, keepdims=True)
    parts_start()

    for n in range(CHUNKS):
        def drain(i, carry):
            wcopy(n, tok, i, to_sib).wait_send()
            return carry

        lax.fori_loop(0, SENDS, drain, 0)

    def drain_a(i, carry):
        acopy(mine, i, to_yd).wait_send()
        return carry

    lax.fori_loop(0, 15, drain_a, 0)
    to_right.wait_send()
    to_left.wait_send()
    kv_copy.wait_send()

    squares_drain()

    parts_wait()
    score = [(parts[4 * s] + parts[4 * s + 1]) + (parts[4 * s + 2] + parts[4 * s + 3]) for s in range(SEC)]
    for s in range(SEC):
        out_ref[s : s + 1] = score[s]
    out_ref[SEC : SEC + 1] = score[1] - score[2] - KL_WEIGHT * (score[3] - score[0])

    parts_drain()


def local(roll_hidden, lengths, norm_gain, w_query, key_value_weight, score_head):
    vmem = pl.BlockSpec(memory_space=pltpu.VMEM)
    smem = pl.BlockSpec(memory_space=pltpu.SMEM)
    hbm = pl.BlockSpec(memory_space=pl.ANY)
    dma = pltpu.SemaphoreType.DMA
    bf16, f32 = jnp.bfloat16, jnp.float32
    out = pl.pallas_call(
        kernel,
        out_shape=jax.ShapeDtypeStruct((SEC + 1, LOCAL_TOKENS), f32),
        in_specs=[smem, hbm, vmem, hbm, hbm, vmem],
        out_specs=vmem,
        scratch_shapes=[
            *(pltpu.VMEM((TOK, PIECE, cols), bf16) for cols in COLS),
            pltpu.VMEM((PIECE, 2, HEAD_SIZE), bf16),
            pltpu.VMEM((2, LOCAL_TOKENS, PIECE), bf16),
            pltpu.VMEM((4, HALF, PIECE), bf16),
            pltpu.VMEM((2, HALF, PIECE), bf16),
            pltpu.VMEM((16, LOCAL_TOKENS, PIECE), bf16),
            pltpu.VMEM((16, LOCAL_TOKENS, PIECE), bf16),
            pltpu.VMEM((16, 1, LOCAL_TOKENS), f32),
            pltpu.VMEM((LOCAL_TOKENS, 128), f32),
            pltpu.VMEM((3, BLOCK, 4 * BLOCK), f32),
            pltpu.VMEM((LOCAL_TOKENS, max(COLS)), f32),
            pltpu.VMEM((LOCAL_TOKENS, sum(COLS[1:])), bf16),
            pltpu.VMEM((2 * LOCAL_TOKENS, 2 * HEAD_SIZE), bf16),
            pltpu.VMEM((LOCAL_TOKENS, HEAD_SIZE), f32),
            pltpu.VMEM((16, 1, LOCAL_TOKENS), f32),
            dma((2,)), dma((CHUNKS,)),
            dma((CHUNKS, SENDS)), dma((CHUNKS, TOK)),
            dma((15,)), dma((16,)),
            dma((2,)), dma((2,)),
            dma((1,)), dma((1,)),
            dma((16,)), dma((16,)),
            dma((16,)), dma((16,)),
        ],
        compiler_params=pltpu.CompilerParams(
            collective_id=0, has_side_effects=True, vmem_limit_bytes=56 * 1024 * 1024
        ),
        name="score_rollouts",
    )(
        lengths, roll_hidden, norm_gain, w_query,
        key_value_weight, score_head,
    )
    return (out[:SEC], out[SEC])


def solution(mesh):
    in_specs = (
        P("tok", None, "tp"),
        P(),
        P("sec", None),
        P("sec", "tok", "tp"),
        P("sec", "tok", None, "tp"),
        P("sec", "tp"),
    )
    out_specs = (P(None, "tok"), P("tok"))
    return jax.shard_map(local, mesh=mesh, in_specs=in_specs, out_specs=out_specs, check_vma=False)
```
